128 devices in a mesh: qgrp: 16 (over z, x), pcol: 8 (over y, core).
Axes of the slice: x: 4, y: 4, z: 4, core: 2. Of those that a mesh axis runs over, the one named last changes fastest.
Arguments:
- queries: bfloat16 [16384, 1024], P('qgrp'), may hold values from -80 to 80
- passages: bfloat16 [131072, 1024], P(('qgrp', 'pcol')), may hold values from -1.5 to 1.5
- block_mask: int32 [2, 16], replicated, may hold values 0 or 1
- positives: int32 [16384], P('qgrp'), may hold values from 0 to 8191
Outputs:
- query_loss: float32 [16384], P('qgrp')
- query_grad: bfloat16 [16384, 1024], P(('qgrp', 'pcol'))
- passage_grad: bfloat16 [131072, 1024], P(('qgrp', 'pcol'))
The draws below stay inside these ranges and needn't reach their ends.
All inputs are finite; a program needn't handle non-finite values.
Results may differ from the reference program's by a relative error of at most 0.017.
Values may be sent and summed in bfloat16 or wider, within the bound.
A program may use at most 128 MiB of HBM per device.

```python
import math
import jax
import jax.numpy as jnp
from jax import lax

D = 1024
QG = 1024
PC = 1024
ROUNDS = 2
NQ = 16384
PB = 8192
NP = 131072
N_QGRP = 16
N_PCOL = 8


quiet_share = 0.25


offset_span = 0.58


def shared_direction(key):
    column = jnp.arange(D, dtype=jnp.int32)
    values = jax.random.truncated_normal(jax.random.fold_in(key, 5), -4.0, 4.0, (D,))
    return jnp.where(column < D // 8, values, 0.0)


def column_damping():
    column = jnp.arange(D, dtype=jnp.int32)
    return jnp.where(column < D // 8, quiet_share, 1.0)


def shard_offset(row_index):
    shard_index = (row_index // PC % N_PCOL).astype(jnp.float32)
    return offset_span * shard_index / (N_PCOL - 1) / (D // 8)


def passage_block(key, scale_low, scale_high):
    direction = shared_direction(key)
    row_index = jnp.arange(NP, dtype=jnp.int32)
    key_spread, key_base = jax.random.split(jax.random.fold_in(key, 7), 2)
    row_scale = jnp.exp(jax.random.uniform(key_spread, (NP,), minval=math.log(scale_low), maxval=math.log(scale_high)))
    base_draw = jax.random.truncated_normal(key_base, -5.0, 5.0, (NP, D)) * column_damping()[None, :]
    return base_draw * (row_scale / math.sqrt(D))[:, None] + shard_offset(row_index)[:, None] * direction[None, :]


def draw_passages(key, part):
    passage_rows = passage_block(key, 0.3, 3.0)
    return jnp.clip(passage_rows, -1.5, 1.5).astype(jnp.bfloat16)


def draw_queries(key, part):
    direction = shared_direction(key)
    key_scale, key_base = jax.random.split(jax.random.fold_in(key, 11), 2)
    row_scale = jnp.exp(jax.random.uniform(key_scale, (NQ,), minval=math.log(0.2), maxval=math.log(0.6)))
    query_draw = jax.random.truncated_normal(key_base, -5.0, 5.0, (NQ, D)) * row_scale[:, None] + 2.0 * direction[None, :]
    return jnp.clip(query_draw, -80.0, 80.0).astype(jnp.bfloat16)


def with_ends(values, own_key, low, high):
    place = [jax.random.randint(jax.random.fold_in(own_key, axis), (), 0, length) for axis, length in enumerate(values.shape)]
    main_axis = values.shape.index(max(values.shape))
    beside = place[:main_axis] + [(place[main_axis] + 1) % values.shape[main_axis]] + place[main_axis + 1:]
    return values.at[tuple(place)].set(low).at[tuple(beside)].set(high)


def setup_inputs(seed: int = 0) -> dict:
    splits = jax.random.split(jax.random.key(seed), 5)
    return {
        "queries": draw_queries(jax.random.fold_in(splits[4], 71), 0),
        "passages": draw_passages(jax.random.fold_in(splits[4], 71), 0),
        "block_mask": with_ends((jax.random.randint(splits[2], (ROUNDS, N_QGRP), 0, 4) < 3).astype(jnp.int32), jax.random.fold_in(splits[2], 1), 0, 1),
        "positives": with_ends(jax.random.randint(splits[3], (NQ,), 0, PB), jax.random.fold_in(splits[3], 1), 0, PB - 1).astype(jnp.int32),
    }


minus_inf = -jnp.inf


def reference(queries, passages, block_mask, positives):
    query_groups = queries.reshape(N_QGRP, QG, D)
    passage_groups = passages.reshape(N_QGRP, PB, D)
    positive_groups = positives.reshape(N_QGRP, QG)

    def per_group(group_index):
        query_rows = query_groups[group_index]
        own_block = passage_groups[group_index]
        round_blocks = [passage_groups[jnp.bitwise_xor(group_index, 1 << round_index)] for round_index in range(ROUNDS)]
        keep_flags = [block_mask[round_index, group_index] > 0 for round_index in range(ROUNDS)]
        own_logits = jnp.dot(query_rows, own_block.T, preferred_element_type=jnp.float32)
        round_logits = [jnp.dot(query_rows, block_rows.T, preferred_element_type=jnp.float32) for block_rows in round_blocks]
        row_maximum = jnp.max(own_logits, axis=1)
        for logits_round, flag_round in zip(round_logits, keep_flags):
            row_maximum = jnp.maximum(row_maximum, jnp.where(flag_round, jnp.max(logits_round, axis=1), minus_inf))
        exp_total = jnp.sum(jnp.exp(own_logits - row_maximum[:, None]), axis=1)
        for logits_round, flag_round in zip(round_logits, keep_flags):
            exp_total = exp_total + jnp.where(flag_round, jnp.sum(jnp.exp(logits_round - row_maximum[:, None]), axis=1), 0.0)
        log_total = row_maximum + jnp.log(exp_total)
        is_positive = jnp.arange(PB, dtype=jnp.int32)[None, :] == positive_groups[group_index][:, None]
        positive_logit = jnp.sum(jnp.where(is_positive, own_logits, 0.0), axis=1)
        group_loss = log_total - positive_logit
        own_weights = (jnp.exp(own_logits - log_total[:, None]) - is_positive.astype(jnp.float32)).astype(jnp.bfloat16)
        round_weights = [jnp.where(flag_round, jnp.exp(logits_round - log_total[:, None]), 0.0).astype(jnp.bfloat16) for logits_round, flag_round in zip(round_logits, keep_flags)]
        group_grad = jnp.dot(own_weights, own_block, preferred_element_type=jnp.float32)
        for weights_round, block_rows in zip(round_weights, round_blocks):
            group_grad = group_grad + jnp.dot(weights_round, block_rows, preferred_element_type=jnp.float32)
        own_grads = jnp.dot(own_weights.T, query_rows, preferred_element_type=jnp.float32)
        round_grads = jnp.stack([jnp.dot(weights_round.T, query_rows, preferred_element_type=jnp.float32) for weights_round in round_weights])
        return group_loss, group_grad.astype(jnp.bfloat16), own_grads, round_grads

    losses, query_grads, own_grads, round_grads = lax.map(per_group, jnp.arange(N_QGRP, dtype=jnp.int32))
    group_ids = jnp.arange(N_QGRP, dtype=jnp.int32)
    passage_grads = own_grads
    for round_index in range(ROUNDS):
        passage_grads = passage_grads + round_grads[jnp.bitwise_xor(group_ids, 1 << round_index), round_index]
    return losses.reshape(NQ), query_grads.reshape(NQ, D), passage_grads.astype(jnp.bfloat16).reshape(NP, D)
```

```python
import functools

import jax
import jax.numpy as jnp
from jax import lax
from jax.experimental import pallas as pl
from jax.experimental.pallas import tpu as pltpu
from jax.sharding import PartitionSpec as P

F32 = jnp.float32
BF16 = jnp.bfloat16
D = 1024
SHARD = 1024
CHIP = 2048
UNIT = 128
BATCH = 256
QUERIES = 512
NB = 2
LOW = -1e30
MESH = pl.DeviceIdType.MESH


def dot_nt(a, b):
    return lax.dot_general(a, b, (((1,), (1,)), ((), ())), preferred_element_type=F32)


def dot_nn(a, b):
    return jnp.dot(a, b, preferred_element_type=F32)


def kernel(
    q_hbm, p_hbm, mask_ref, pos_ref,
    loss_ref, qg_ref, pg_hbm,
    qv, pv, pt, lg, ev, tf, t0,
    sb, rb, sa, ra, sy, ry, acc,
    pgs, pgr, pgo, pgv,
    st, sty, stc, stx, sc, ls, lr,
    load_sem, out_sem, pair_send, pair_recv,
    qa_send, qa_recv, qb_send, qb_recv, qy_send, qy_recv,
    sty_send, sty_recv, stx_send, stx_recv,
    tb_send, tb_recv, ta_send, ta_recv, ty_send, ty_recv,
):
    g = lax.axis_index("qgrp")
    k = lax.axis_index("pcol")
    x = lax.rem(g, 4)
    y = lax.div(k, 2)
    c = lax.rem(k, 2)
    h = lax.rem(y, 2)
    g1 = g + 1 - 2 * lax.rem(x, 2)
    g2 = g + 2 - 4 * lax.div(x, 2)
    g3 = g + 3 - 2 * x
    up = (g, lax.rem(k + 2, 8))
    far = (g, lax.rem(k + 4, 8))
    down = (g, lax.rem(k + 6, 8))
    pair = (g, k + 1 - 2 * c)
    n1, n2, n3 = (g1, k), (g2, k), (g3, k)

    def rcopy(src, dst, ssem, rsem, dev):
        return pltpu.make_async_remote_copy(
            src_ref=src, dst_ref=dst, send_sem=ssem, recv_sem=rsem,
            device_id=dev, device_id_type=MESH,
        )

    q_load = pltpu.make_async_copy(q_hbm.at[:, c], qv.at[0], load_sem.at[0])
    p_load = pltpu.make_async_copy(p_hbm, pv.at[0], load_sem.at[1])
    q_load.start()
    p_load.start()

    barrier = pltpu.get_barrier_semaphore()
    for dev in (up, far, down, pair, n1, n2, n3):
        pl.semaphore_signal(barrier, inc=1, device_id=dev, device_id_type=MESH)
    pl.semaphore_wait(barrier, 7)

    p_swap = rcopy(p_hbm, pv.at[1], pair_send.at[0], pair_recv.at[0], pair)
    sends = [p_swap]

    def start(copy):
        copy.start()
        sends.append(copy)

    def rows(s):
        return pl.ds(64 * s, 64)

    def qa(b, s):
        return rcopy(
            q_hbm.at[2 * b + h, c, rows(s)], qv.at[1, 2 * b + h, rows(s)],
            qa_send.at[b, s], qa_recv.at[b, s], n1,
        )

    def qb(b, s):
        return rcopy(
            qv.at[1, 2 * b + h, rows(s)], qv.at[2, 2 * b + h, rows(s)],
            qb_send.at[b, s], qb_recv.at[b, s], n3,
        )

    def qy(b, r, s):
        return rcopy(
            qv.at[1 + r, 2 * b + h, rows(s)], qv.at[1 + r, 2 * b + h, rows(s)],
            qy_send.at[b, r, s], qy_recv.at[b, r, s], (up, down)[s],
        )

    def qy_wait(b, r):
        for s in range(2):
            block = qv.at[1 + r, 2 * b + 1 - h, rows(s)]
            rcopy(
                block, block, qy_send.at[b, r, s], qy_recv.at[b, r, s], (up, down)[s]
            ).wait_recv()

    for b in range(NB):
        for s in range(2):
            start(qa(b, s))
    p_swap.start()

    def forward_a(b):
        for s in range(2):
            qa(b, s).wait_recv()
            start(qb(b, s))
            start(qy(b, 0, s))

    def forward_b(b):
        for s in range(2):
            qb(b, s).wait_recv()
            start(qy(b, 1, s))

    flags = [mask_ref[0, g1] > 0, mask_ref[1, g2] > 0]

    def positive_row(b):
        return jnp.concatenate(
            [pos_ref[pl.ds(2 * (2 * b + j) + c, 1), :] for j in range(2)], axis=1
        )

    def first_column(half):
        return (k if half == 0 else k + 1 - 2 * c) * SHARD

    ls[...] = jnp.zeros((8, UNIT), F32)
    q_load.wait()
    p_load.wait()
    own_max = jnp.full((1, QUERIES), LOW, F32)

    def own_logits(half, peak):
        def body(i, peak):
            own_queries = qv[0].reshape(QUERIES, D)
            block = dot_nt(pv[half, pl.ds(i * 512, 512), :], own_queries)
            lg[pl.ds(half * SHARD + i * 512, 512), :] = block
            return jnp.maximum(peak, jnp.max(block, axis=0, keepdims=True))

        return lax.fori_loop(0, 2, body, peak)

    own_max = own_logits(0, own_max)
    forward_a(0)
    p_swap.wait_recv()
    own_max = own_logits(1, own_max)
    forward_b(0)

    positive_all = jnp.concatenate([positive_row(b) for b in range(NB)], axis=1)

    def own_exp(half, carry):
        def body(i, carry):
            total, positive = carry
            r = half * SHARD + i * 256
            block = lg[pl.ds(r, 256), :]
            column = lax.broadcasted_iota(jnp.int32, (256, QUERIES), 0) + (
                first_column(half) + i * 256
            )
            e = jnp.exp(block - own_max)
            ev[0, pl.ds(r, 256), :] = e.astype(BF16)
            total = total + jnp.sum(e, axis=0, keepdims=True)
            positive = positive + jnp.sum(
                jnp.where(column == positive_all, block, 0.0), axis=0, keepdims=True
            )
            return total, positive

        return lax.fori_loop(0, 4, body, carry)

    zero = jnp.zeros((1, QUERIES), F32)
    own_total, own_positive = own_exp(1, own_exp(0, (zero, zero)))
    for b in range(NB):
        part = slice(b * BATCH, (b + 1) * BATCH)
        st[b, 0:1, :] = own_max[:, part]
        st[b, 3:4, :] = own_total[:, part]
        st[b, 6:7, :] = own_positive[:, part]
        st[b, 7:8, :] = jnp.zeros((1, BATCH), F32)

    for half in range(2):
        @pl.loop(0, 4)
        def _(i):
            pt[half * 4 + i] = pv[half, pl.ds(i * 256, 256), :].T

    forward_a(1)

    def lent(b, r):
        def body(i, peak):
            queries = qv[1 + r, 2 * b:2 * b + 2].reshape(BATCH, D)
            half, rest = lax.div(i, 2), lax.rem(i, 2)
            block = dot_nt(pv[half, pl.ds(rest * 512, 512), :], queries)
            lg[pl.ds(i * 512, 512), 0:BATCH] = block
            return jnp.maximum(peak, jnp.max(block, axis=0, keepdims=True))

        peak = lax.fori_loop(0, 4, body, jnp.full((1, BATCH), LOW, F32))

        def exp_body(i, total):
            e = jnp.exp(lg[pl.ds(i * 256, 256), 0:BATCH] - peak)
            ev[1 + r, pl.ds(i * 256, 256), b * BATCH:(b + 1) * BATCH] = e.astype(BF16)
            return total + jnp.sum(e, axis=0, keepdims=True)

        total = lax.fori_loop(0, 8, exp_body, jnp.zeros((1, BATCH), F32))
        st[b, 1 + r:2 + r, :] = jnp.where(flags[r], peak, LOW)
        st[b, 4 + r:5 + r, :] = total

    def stats_y(b, i):
        dev = (down, far, up)[i]
        return rcopy(st.at[b], sty.at[b, i], sty_send.at[b, i], sty_recv.at[b, i], dev)

    def stats_x(b, i):
        dev = (n1, n2, n3)[i]
        return rcopy(stc.at[b], stx.at[b, i], stx_send.at[b, i], stx_recv.at[b, i], dev)

    def combine_y(b):
        for i in range(3):
            stats_y(b, i).wait_recv()
        peaks = [st[b, 0:3, :]] + [sty[b, i, 0:3, :] for i in range(3)]
        sums = [st[b, 3:6, :]] + [sty[b, i, 3:6, :] for i in range(3)]
        peak = functools.reduce(jnp.maximum, peaks)
        total = sum(s * jnp.exp(m - peak) for s, m in zip(sums, peaks))
        positive = st[b, 6:7, :] + sty[b, 0, 6:7, :] + sty[b, 1, 6:7, :] + sty[b, 2, 6:7, :]
        stc[b, 0:3, :] = peak
        stc[b, 3:6, :] = total
        stc[b, 6:7, :] = positive
        stc[b, 7:8, :] = jnp.zeros((1, BATCH), F32)

    def combine_x(b):
        for i in range(3):
            stats_x(b, i).wait_recv()
        own, one, two, three = stc[b], stx[b, 0], stx[b, 1], stx[b, 2]
        sources = (
            ((own, 0), (one, 1), (two, 2)),
            ((one, 0), (own, 1), (three, 2)),
            ((two, 0), (own, 2), (three, 1)),
        )
        log_totals = []
        for source in sources:
            peaks = [a[r:r + 1] for a, r in source]
            sums = [a[3 + r:4 + r] for a, r in source]
            peak = functools.reduce(jnp.maximum, peaks)
            total = sum(s * jnp.exp(m - peak) for s, m in zip(sums, peaks))
            log_totals.append(peak + jnp.log(total))
        for r in range(3):
            sc[b, r:r + 1, :] = jnp.exp(st[b, r:r + 1, :] - log_totals[r])
        positive = own[6:7]
        sc[b, 3:4, :] = jnp.exp(positive - log_totals[0]) - 1.0
        loss = log_totals[0] - positive
        for j in range(2):
            ls[2 * b + j:2 * b + j + 1, :] = loss[:, j * UNIT:(j + 1) * UNIT]

    def terms(b, r):
        @pl.loop(0, 4)
        def _(i):
            total = None
            for n in range(8):
                part = dot_nn(
                    pt[n, pl.ds(i * 256, 256), :],
                    ev[r, n * 256:(n + 1) * 256, b * BATCH:(b + 1) * BATCH],
                )
                total = part if total is None else total + part
            if r == 0:
                t0[b, pl.ds(i * 256, 256), :] = total
            else:
                tf[b, r - 1, pl.ds(i * 256, 256), :] = total

    def own_weights(b):
        scale, less = sc[b, 0:1, :], sc[b, 3:4, :]
        where = positive_row(b)
        for half in range(2):
            @pl.loop(0, 4)
            def _(i):
                span = pl.ds(half * SHARD + i * 256, 256)
                column = lax.broadcasted_iota(jnp.int32, (256, BATCH), 0) + (
                    first_column(half) + i * 256
                )
                e = ev[0, span, b * BATCH:(b + 1) * BATCH].astype(F32)
                w = jnp.where(column == where, less, e * scale)
                ev[0, span, b * BATCH:(b + 1) * BATCH] = w.astype(BF16)

    def lent_weights(b, r):
        scale = sc[b, 1 + r:2 + r, :]

        @pl.loop(0, 8)
        def _(i):
            span = pl.ds(i * 256, 256)
            e = ev[1 + r, span, b * BATCH:(b + 1) * BATCH].astype(F32)
            ev[1 + r, span, b * BATCH:(b + 1) * BATCH] = (e * scale).astype(BF16)

    def tb(b, j):
        return rcopy(sb.at[b, j], rb.at[b, j], tb_send.at[b, j], tb_recv.at[b, j], n3)

    def ta(b, j):
        return rcopy(sa.at[b, j], ra.at[b, j], ta_send.at[b, j], ta_recv.at[b, j], n1)

    def ty(b, j):
        unit = 2 * b + j
        slot = lax.rem(y - unit + 4, 4) - 1
        return rcopy(
            sy.at[b, j], ry.at[slot], ty_send.at[b, j], ty_recv.at[slot], (g, 2 * unit + c)
        )

    def lanes(j):
        return slice(j * UNIT, (j + 1) * UNIT)

    def send_b(b):
        for j in range(2):
            sb[b, j] = (tf[b, 1, :, lanes(j)] * sc[b, 2:3, lanes(j)]).astype(BF16)
            start(tb(b, j))

    def send_a(b):
        for j in range(2):
            tb(b, j).wait_recv()
            sa[b, j] = (
                tf[b, 0, :, lanes(j)] * sc[b, 1:2, lanes(j)] + rb[b, j].astype(F32)
            ).astype(BF16)
            start(ta(b, j))

    def send_y(b):
        for j in range(2):
            unit = 2 * b + j
            ta(b, j).wait_recv()

            @pl.when(y == unit)
            def _():
                acc[...] = t0[b, :, lanes(j)] + ra[b, j].astype(F32)

            @pl.when(y != unit)
            def _():
                sy[b, j] = (t0[b, :, lanes(j)] + ra[b, j].astype(F32)).astype(BF16)
                ty(b, j).start()

    def passage_part(half, target):
        @pl.loop(0, 4)
        def _(i):
            total = None
            for r in range(3):
                part = dot_nn(
                    ev[r, pl.ds(half * SHARD + i * 256, 256), :], qv[r].reshape(QUERIES, D)
                )
                total = part if total is None else total + part
            target[pl.ds(i * 256, 256), :] = total.astype(target.dtype)

    qy_wait(0, 0)
    lent(0, 0)
    forward_b(1)
    qy_wait(0, 1)
    lent(0, 1)
    for i in range(3):
        start(stats_y(0, i))
    terms(0, 2)
    combine_y(0)
    for i in range(3):
        start(stats_x(0, i))
    terms(0, 1)
    combine_x(0)
    send_b(0)
    qy_wait(1, 0)
    lent(1, 0)
    qy_wait(1, 1)
    lent(1, 1)
    for i in range(3):
        start(stats_y(1, i))
    terms(1, 2)
    combine_y(1)
    for i in range(3):
        start(stats_x(1, i))
    terms(1, 1)
    combine_x(1)
    send_b(1)
    loss_copy = rcopy(ls, lr, pair_send.at[1], pair_recv.at[1], pair)
    start(loss_copy)
    send_a(0)
    own_weights(0)
    terms(0, 0)
    own_weights(1)
    terms(1, 0)
    for b in range(NB):
        for r in range(2):
            lent_weights(b, r)
    send_a(1)
    send_y(0)
    passage_part(1, pgs)
    pg_copy = rcopy(pgs, pgr, pair_send.at[2], pair_recv.at[2], pair)
    start(pg_copy)
    passage_part(0, pgo)
    send_y(1)
    loss_copy.wait_recv()
    for j in range(4):
        loss_ref[pl.ds(2 * j + c, 1), :] = ls[j:j + 1, :]
        loss_ref[pl.ds(2 * j + 1 - c, 1), :] = lr[j:j + 1, :]
    pg_copy.wait_recv()
    outs = []
    for i in range(4):
        span = pl.ds(i * 256, 256)
        pgv[span, :] = (pgo[span, :] + pgr[span, :].astype(F32)).astype(BF16)
        out = pltpu.make_async_copy(pgv.at[span], pg_hbm.at[span], out_sem.at[i])
        out.start()
        outs.append(out)
    total = acc[...]
    for slot in range(3):
        rcopy(sy.at[0, 0], ry.at[slot], ty_send.at[0, 0], ty_recv.at[slot], up).wait_recv()
        total = total + ry[slot].astype(F32)
    qg_ref[...] = total.T.astype(BF16)
    for copy in sends:
        copy.wait_send()
    for b in range(NB):
        for j in range(2):
            @pl.when(y != 2 * b + j)
            def _():
                ty(b, j).wait_send()
    for out in outs:
        out.wait()


def on_device(queries, passages, block_mask, positives):
    vmem = pltpu.VMEM
    dma = pltpu.SemaphoreType.DMA
    loss, query_grad, passage_grad = pl.pallas_call(
        kernel,
        out_shape=(
            jax.ShapeDtypeStruct((8, 128), F32),
            jax.ShapeDtypeStruct((UNIT, D), BF16),
            jax.ShapeDtypeStruct((SHARD, D), BF16),
        ),
        in_specs=[
            pl.BlockSpec(memory_space=pl.ANY),
            pl.BlockSpec(memory_space=pl.ANY),
            pl.BlockSpec(memory_space=pltpu.SMEM),
            pl.BlockSpec(memory_space=pltpu.VMEM),
        ],
        out_specs=(
            pl.BlockSpec(memory_space=pltpu.VMEM),
            pl.BlockSpec(memory_space=pltpu.VMEM),
            pl.BlockSpec(memory_space=pl.ANY),
        ),
        scratch_shapes=[
            vmem((3, 4, UNIT, D), BF16),
            vmem((2, SHARD, D), BF16),
            vmem((8, D, 256), BF16),
            vmem((CHIP, QUERIES), F32),
            vmem((3, CHIP, QUERIES), BF16),
            vmem((NB, 2, D, BATCH), F32),
            vmem((NB, D, BATCH), F32),
            vmem((NB, 2, D, UNIT), BF16),
            vmem((NB, 2, D, UNIT), BF16),
            vmem((NB, 2, D, UNIT), BF16),
            vmem((NB, 2, D, UNIT), BF16),
            vmem((NB, 2, D, UNIT), BF16),
            vmem((3, D, UNIT), BF16),
            vmem((D, UNIT), F32),
            vmem((SHARD, D), BF16),
            vmem((SHARD, D), BF16),
            vmem((SHARD, D), F32),
            vmem((SHARD, D), BF16),
            vmem((NB, 8, BATCH), F32),
            vmem((NB, 3, 8, BATCH), F32),
            vmem((NB, 8, BATCH), F32),
            vmem((NB, 3, 8, BATCH), F32),
            vmem((NB, 8, BATCH), F32),
            vmem((8, UNIT), F32),
            vmem((8, UNIT), F32),
            dma((2,)), dma((4,)), dma((3,)), dma((3,)),
            dma((NB, 2)), dma((NB, 2)), dma((NB, 2)), dma((NB, 2)),
            dma((NB, 2, 2)), dma((NB, 2, 2)),
            dma((NB, 3)), dma((NB, 3)), dma((NB, 3)), dma((NB, 3)),
            dma((NB, 2)), dma((NB, 2)), dma((NB, 2)), dma((NB, 2)),
            dma((NB, 2)), dma((3,)),
        ],
        compiler_params=pltpu.CompilerParams(
            collective_id=0, has_side_effects=True, vmem_limit_bytes=60 * 1024 * 1024
        ),
        cost_estimate=pl.CostEstimate(
            flops=9 * 2 * 1024**3, bytes_accessed=7 * 2**20, transcendentals=3 * 2**20
        ),
    )(
        queries.reshape(4, 2, UNIT, D),
        passages,
        block_mask,
        positives.reshape(8, UNIT),
    )
    return loss.reshape(1024), query_grad, passage_grad


def solution(mesh):
    in_specs = (P("qgrp", None), P(("qgrp", "pcol"), None), P(), P("qgrp"))
    out_specs = (P("qgrp"), P(("qgrp", "pcol"), None), P(("qgrp", "pcol"), None))
    return jax.shard_map(
        on_device, mesh=mesh, in_specs=in_specs, out_specs=out_specs, check_vma=False
    )
```

```python
import functools

import jax
import jax.numpy as jnp
from jax import lax
from jax.experimental import pallas as pl
from jax.experimental.pallas import tpu as pltpu
from jax.sharding import PartitionSpec as P

F32 = jnp.float32
BF16 = jnp.bfloat16
D = 1024
SHARD = 1024
CHIP = 2048
UNIT = 128
BATCH = 256
QUERIES = 512
NB = 2
PIECES = 4
HALF = 512
LOW = -1e30
MESH = pl.DeviceIdType.MESH


def dot_nt(a, b):
    return lax.dot_general(a, b, (((1,), (1,)), ((), ())), preferred_element_type=F32)


def dot_nn(a, b):
    return jnp.dot(a, b, preferred_element_type=F32)


def kernel(
    q_hbm, p_hbm, mask_ref, pos_ref,
    loss_ref, qg_ref, pg_hbm,
    qv, pv, pt, lg, ev, t1, t0,
    sb, rb, sa, ra, sy, ry, acc,
    pgs, pgr, pgo, pgv,
    st, sty, stm, stc, stx, sc, ls, lr,
    load_sem, out_sem, pair_send, pair_recv,
    qa_send, qa_recv, qb_send, qb_recv, qy_send, qy_recv,
    sty_send, sty_recv, stx_send, stx_recv, stm_send, stm_recv,
    tb_send, tb_recv, ta_send, ta_recv, ty_send, ty_recv,
):
    g = lax.axis_index("qgrp")
    k = lax.axis_index("pcol")
    x = lax.rem(g, 4)
    y = lax.div(k, 2)
    c = lax.rem(k, 2)
    h = lax.rem(y, 2)
    g1 = g + 1 - 2 * lax.rem(x, 2)
    g2 = g + 2 - 4 * lax.div(x, 2)
    g3 = g + 3 - 2 * x
    up = (g, lax.rem(k + 2, 8))
    far = (g, lax.rem(k + 4, 8))
    down = (g, lax.rem(k + 6, 8))
    pair = (g, k + 1 - 2 * c)
    n1, n2, n3 = (g1, k), (g2, k), (g3, k)

    def rcopy(src, dst, ssem, rsem, dev):
        return pltpu.make_async_remote_copy(
            src_ref=src, dst_ref=dst, send_sem=ssem, recv_sem=rsem,
            device_id=dev, device_id_type=MESH,
        )

    loads = [pltpu.make_async_copy(p_hbm, pv.at[0], load_sem.at[NB * 2])]
    for b in range(NB):
        for j in range(2):
            slot = 2 * b + j
            loads.append(
                pltpu.make_async_copy(q_hbm.at[b + 2 * j, c], qv.at[0, slot], load_sem.at[slot])
            )
    for copy in loads:
        copy.start()

    barrier = pltpu.get_barrier_semaphore()
    for dev in (up, far, down, pair, n1, n2, n3):
        pl.semaphore_signal(barrier, inc=1, device_id=dev, device_id_type=MESH)
    pl.semaphore_wait(barrier, 7)

    p_swap = rcopy(p_hbm, pv.at[1], pair_send.at[0], pair_recv.at[0], pair)
    sends = [p_swap]

    def start(copy):
        copy.start()
        sends.append(copy)

    def rows(i):
        return pl.ds(64 * (i % 2) + 32 * (i // 2), 32)

    def qa(b, i):
        return rcopy(
            q_hbm.at[b + 2 * h, c, rows(i)], qv.at[1, 2 * b + h, rows(i)],
            qa_send.at[b, i], qa_recv.at[b, i], n1,
        )

    def qb(b, i):
        return rcopy(
            qv.at[1, 2 * b + h, rows(i)], qv.at[2, 2 * b + h, rows(i)],
            qb_send.at[b, i], qb_recv.at[b, i], n3,
        )

    def qy(b, r, i):
        block = qv.at[1 + r, 2 * b + h, rows(i)]
        return rcopy(
            block, block, qy_send.at[b, r, i], qy_recv.at[b, r, i], (up, down)[i % 2]
        )

    def qy_wait(b, r):
        for i in range(PIECES):
            block = qv.at[1 + r, 2 * b + 1 - h, rows(i)]
            rcopy(
                block, block, qy_send.at[b, r, i], qy_recv.at[b, r, i], (up, down)[i % 2]
            ).wait_recv()

    for b in range(NB):
        for i in range(PIECES):
            start(qa(b, i))
    p_swap.start()

    def forward_a(b, i):
        qa(b, i).wait_recv()
        start(qb(b, i))
        start(qy(b, 0, i))

    def forward_b(b, i):
        qb(b, i).wait_recv()
        start(qy(b, 1, i))

    flags = [mask_ref[0, g1] > 0, mask_ref[1, g2] > 0]

    def positive_row(b):
        return jnp.concatenate(
            [pos_ref[pl.ds(2 * (b + 2 * j) + c, 1), :] for j in range(2)], axis=1
        )

    def first_column(half):
        return (k if half == 0 else k + 1 - 2 * c) * SHARD

    ls[...] = jnp.zeros((8, UNIT), F32)
    for copy in loads:
        copy.wait()
    own_max = jnp.full((1, QUERIES), LOW, F32)

    def own_logits(half, peak):
        def body(i, peak):
            own_queries = qv[0].reshape(QUERIES, D)
            block = dot_nt(pv[half, pl.ds(i * 512, 512), :], own_queries)
            lg[pl.ds(half * SHARD + i * 512, 512), :] = block
            return jnp.maximum(peak, jnp.max(block, axis=0, keepdims=True))

        return lax.fori_loop(0, 2, body, peak)

    def transpose(half):
        for i in range(4):
            first = half * SHARD + i * 256
            pt[:, first:first + 256] = pv[half, pl.ds(i * 256, 256), :].T

    own_max = own_logits(0, own_max)
    transpose(0)
    forward_a(0, 0)
    forward_a(0, 1)
    p_swap.wait_recv()
    own_max = own_logits(1, own_max)
    forward_a(0, 2)
    forward_b(0, 0)
    forward_a(0, 3)
    forward_b(0, 1)
    transpose(1)
    forward_a(1, 0)
    forward_b(0, 2)

    positive_all = jnp.concatenate([positive_row(b) for b in range(NB)], axis=1)

    def own_exp(half, carry):
        def body(i, carry):
            total, positive = carry
            r = half * SHARD + i * 256
            block = lg[pl.ds(r, 256), :]
            column = lax.broadcasted_iota(jnp.int32, (256, QUERIES), 0) + (
                first_column(half) + i * 256
            )
            e = jnp.exp(block - own_max)
            ev[0, pl.ds(r, 256), :] = e.astype(BF16)
            total = total + jnp.sum(e, axis=0, keepdims=True)
            positive = positive + jnp.sum(
                jnp.where(column == positive_all, block, 0.0), axis=0, keepdims=True
            )
            return total, positive

        return lax.fori_loop(0, 4, body, carry)

    zero = jnp.zeros((1, QUERIES), F32)
    own_sums = own_exp(0, (zero, zero))
    forward_a(1, 1)
    forward_b(0, 3)
    own_total, own_positive = own_exp(1, own_sums)
    for b in range(NB):
        part = slice(b * BATCH, (b + 1) * BATCH)
        st[b, 0:1, :] = own_max[:, part]
        st[b, 3:4, :] = own_total[:, part]
        st[b, 6:7, :] = own_positive[:, part]
        st[b, 7:8, :] = jnp.zeros((1, BATCH), F32)

    def lent(b, r):
        def body(half, peak):
            queries = qv[1 + r, 2 * b:2 * b + 2].reshape(BATCH, D)
            block = dot_nt(pv[half], queries)
            lg[pl.ds(half * SHARD, SHARD), 0:BATCH] = block
            return jnp.maximum(peak, jnp.max(block, axis=0, keepdims=True))

        peak = lax.fori_loop(0, 2, body, jnp.full((1, BATCH), LOW, F32))

        def exp_body(i, total):
            e = jnp.exp(lg[pl.ds(i * 256, 256), 0:BATCH] - peak)
            ev[1 + r, pl.ds(i * 256, 256), b * BATCH:(b + 1) * BATCH] = e.astype(BF16)
            return total + jnp.sum(e, axis=0, keepdims=True)

        total = lax.fori_loop(0, 8, exp_body, jnp.zeros((1, BATCH), F32))
        st[b, 1 + r:2 + r, :] = jnp.where(flags[r], peak, LOW)
        st[b, 4 + r:5 + r, :] = total

    def stats_y(b, i):
        dev = (down, far, up)[i]
        return rcopy(st.at[b], sty.at[b, i], sty_send.at[b, i], sty_recv.at[b, i], dev)

    def stats_m(b):
        return rcopy(st.at[b], stm.at[b], stm_send.at[b], stm_recv.at[b], n3)

    def stats_x(b, i):
        dev = (n1, n2, n3)[i]
        return rcopy(stc.at[b], stx.at[b, i], stx_send.at[b, i], stx_recv.at[b, i], dev)

    def combine_y(b):
        for i in range(3):
            stats_y(b, i).wait_recv()
        peaks = [st[b, 0:3, :]] + [sty[b, i, 0:3, :] for i in range(3)]
        sums = [st[b, 3:6, :]] + [sty[b, i, 3:6, :] for i in range(3)]
        peak = functools.reduce(jnp.maximum, peaks)
        total = sum(s * jnp.exp(m - peak) for s, m in zip(sums, peaks))
        positive = st[b, 6:7, :] + sty[b, 0, 6:7, :] + sty[b, 1, 6:7, :] + sty[b, 2, 6:7, :]
        stc[b, 0:3, :] = peak
        stc[b, 3:6, :] = total
        stc[b, 6:7, :] = positive
        stc[b, 7:8, :] = jnp.zeros((1, BATCH), F32)

    def combine_x(b):
        for i in range(3):
            stats_x(b, i).wait_recv()
        own, one, two, three = stc[b], stx[b, 0], stx[b, 1], stx[b, 2]
        sources = (
            ((own, 0), (one, 1), (two, 2)),
            ((one, 0), (own, 1), (three, 2)),
            ((two, 0), (own, 2), (three, 1)),
        )
        log_totals = []
        for source in sources:
            peaks = [a[r:r + 1] for a, r in source]
            sums = [a[3 + r:4 + r] for a, r in source]
            peak = functools.reduce(jnp.maximum, peaks)
            total = sum(s * jnp.exp(m - peak) for s, m in zip(sums, peaks))
            log_totals.append(peak + jnp.log(total))
        for r in range(3):
            sc[b, r:r + 1, :] = jnp.exp(st[b, r:r + 1, :] - log_totals[r])
        stats_m(b).wait_recv()
        sc[b, 4:5, :] = jnp.exp(stm[b, 2:3, :] - log_totals[1])
        positive = own[6:7]
        sc[b, 3:4, :] = jnp.exp(positive - log_totals[0]) - 1.0
        loss = log_totals[0] - positive
        for j in range(2):
            ls[b + 2 * j:b + 2 * j + 1, :] = loss[:, j * UNIT:(j + 1) * UNIT]

    def term(b, r, i):
        return dot_nn(pt[pl.ds(i * HALF, HALF), :], ev[r, :, b * BATCH:(b + 1) * BATCH])

    def terms(b, r):
        target = t0 if r == 0 else t1

        @pl.loop(0, 2)
        def _(i):
            target[b, pl.ds(i * HALF, HALF), :] = term(b, r, i)

    def own_weights(b):
        scale, less = sc[b, 0:1, :], sc[b, 3:4, :]
        where = positive_row(b)
        for half in range(2):
            @pl.loop(0, 4)
            def _(i):
                span = pl.ds(half * SHARD + i * 256, 256)
                column = lax.broadcasted_iota(jnp.int32, (256, BATCH), 0) + (
                    first_column(half) + i * 256
                )
                e = ev[0, span, b * BATCH:(b + 1) * BATCH].astype(F32)
                w = jnp.where(column == where, less, e * scale)
                ev[0, span, b * BATCH:(b + 1) * BATCH] = w.astype(BF16)

    def lent_weights(b, r):
        scale = sc[b, 1 + r:2 + r, :]

        @pl.loop(0, 8)
        def _(i):
            span = pl.ds(i * 256, 256)
            e = ev[1 + r, span, b * BATCH:(b + 1) * BATCH].astype(F32)
            ev[1 + r, span, b * BATCH:(b + 1) * BATCH] = (e * scale).astype(BF16)

    def part(n):
        return n % 2, pl.ds(HALF * (n // 2), HALF)

    def tb(b, n):
        j, d = part(n)
        return rcopy(
            sb.at[b, j, d], rb.at[b, j, d], tb_send.at[b, n], tb_recv.at[b, n], n3
        )

    def ta(b, n):
        j, d = part(n)
        return rcopy(
            sa.at[b, j, d], ra.at[b, j, d], ta_send.at[b, n], ta_recv.at[b, n], n1
        )

    def ty(b, n):
        j, d = part(n)
        unit = b + 2 * j
        slot = lax.rem(y - unit + 4, 4) - 1
        return rcopy(
            sy.at[b, j, d], ry.at[slot, d], ty_send.at[b, n], ty_recv.at[slot, n // 2],
            (g, 2 * unit + c),
        )

    def lanes(j):
        return slice(j * UNIT, (j + 1) * UNIT)

    def send_b(b, i):
        total = term(b, 2, i).astype(BF16)
        for j in range(2):
            sb[b, j, pl.ds(i * HALF, HALF), :] = total[:, lanes(j)]
            start(tb(b, 2 * i + j))

    def send_a(b, n):
        j, d = part(n)
        tb(b, n).wait_recv()
        sa[b, j, d] = (
            t1[b, d, lanes(j)] * sc[b, 1:2, lanes(j)]
            + rb[b, j, d].astype(F32) * sc[b, 4:5, lanes(j)]
        ).astype(BF16)
        start(ta(b, n))

    def send_y(b, n):
        j, d = part(n)
        unit = b + 2 * j
        ta(b, n).wait_recv()

        @pl.when(y == unit)
        def _():
            acc[d] = t0[b, d, lanes(j)] + ra[b, j, d].astype(F32)

        @pl.when(y != unit)
        def _():
            sy[b, j, d] = (t0[b, d, lanes(j)] + ra[b, j, d].astype(F32)).astype(BF16)
            ty(b, n).start()

    def passage_part(half, i, target):
        total = None
        for r in range(3):
            add = dot_nn(
                ev[r, pl.ds(half * SHARD + i * 512, 512), :], qv[r].reshape(QUERIES, D)
            )
            total = add if total is None else total + add
        target[pl.ds(i * 512, 512), :] = total.astype(target.dtype)

    def begin_stats(b):
        start(stats_m(b))
        for i in range(3):
            start(stats_y(b, i))

    def begin_stats_x(b):
        combine_y(b)
        for i in range(3):
            start(stats_x(b, i))

    qy_wait(0, 0)
    lent(0, 0)
    forward_a(1, 2)
    forward_b(1, 0)
    forward_a(1, 3)
    forward_b(1, 1)
    qy_wait(0, 1)
    lent(0, 1)
    begin_stats(0)
    send_b(0, 0)
    forward_b(1, 2)
    send_b(0, 1)
    forward_b(1, 3)
    begin_stats_x(0)
    terms(0, 1)
    qy_wait(1, 0)
    lent(1, 0)
    combine_x(0)
    send_a(0, 0)
    qy_wait(1, 1)
    lent(1, 1)
    begin_stats(1)
    send_a(0, 1)
    send_b(1, 0)
    send_b(1, 1)
    send_a(0, 2)
    own_weights(0)
    terms(0, 0)
    send_a(0, 3)
    begin_stats_x(1)
    send_y(0, 0)
    send_y(0, 1)
    terms(1, 1)
    lent_weights(0, 0)
    lent_weights(0, 1)
    combine_x(1)
    loss_copy = rcopy(ls, lr, pair_send.at[1], pair_recv.at[1], pair)
    start(loss_copy)
    send_y(0, 2)
    send_a(1, 0)
    own_weights(1)
    terms(1, 0)
    send_a(1, 1)
    send_y(0, 3)
    lent_weights(1, 0)
    lent_weights(1, 1)
    passage_part(1, 0, pgs)
    send_a(1, 2)
    passage_part(1, 1, pgs)
    pg_copy = rcopy(pgs, pgr, pair_send.at[2], pair_recv.at[2], pair)
    start(pg_copy)
    send_a(1, 3)
    send_y(1, 0)
    passage_part(0, 0, pgo)
    send_y(1, 1)
    passage_part(0, 1, pgo)
    send_y(1, 2)
    send_y(1, 3)
    loss_copy.wait_recv()
    for j in range(4):
        loss_ref[pl.ds(2 * j + c, 1), :] = ls[j:j + 1, :]
        loss_ref[pl.ds(2 * j + 1 - c, 1), :] = lr[j:j + 1, :]
    pg_copy.wait_recv()
    outs = []
    for i in range(4):
        span = pl.ds(i * 256, 256)
        pgv[span, :] = (pgo[span, :] + pgr[span, :].astype(F32)).astype(BF16)
        out = pltpu.make_async_copy(pgv.at[span], pg_hbm.at[span], out_sem.at[i])
        out.start()
        outs.append(out)
    for i in range(2):
        d = slice(i * HALF, (i + 1) * HALF)
        total = acc[d]
        for slot in range(3):
            rcopy(
                sy.at[0, 0, d], ry.at[slot, d], ty_send.at[0, 0], ty_recv.at[slot, i], up
            ).wait_recv()
            total = total + ry[slot, d].astype(F32)
        qg_ref[:, d] = total.T.astype(BF16)
    for copy in sends:
        copy.wait_send()
    for b in range(NB):
        for n in range(4):
            @pl.when(y != b + 2 * (n % 2))
            def _():
                ty(b, n).wait_send()
    for out in outs:
        out.wait()


def finish(loss_in, qg_in, pg_in, loss_out, qg_out, pg_out, sems):
    copies = [
        pltpu.make_async_copy(loss_in, loss_out, sems.at[4]),
        pltpu.make_async_copy(qg_in, qg_out, sems.at[5]),
    ]
    for i in range(4):
        span = pl.ds(i * 256, 256)
        copies.append(pltpu.make_async_copy(pg_in.at[span], pg_out.at[span], sems.at[i]))
    for copy in copies:
        copy.start()
    for copy in copies:
        copy.wait()


def on_device(queries, passages, block_mask, positives):
    vmem = pltpu.VMEM
    dma = pltpu.SemaphoreType.DMA
    loss, query_grad, passage_grad = pl.pallas_call(
        kernel,
        out_shape=(
            jax.ShapeDtypeStruct((8, 128), F32),
            jax.ShapeDtypeStruct((UNIT, D), BF16),
            jax.ShapeDtypeStruct((SHARD, D), BF16),
        ),
        in_specs=[
            pl.BlockSpec(memory_space=pl.ANY),
            pl.BlockSpec(memory_space=pl.ANY),
            pl.BlockSpec(memory_space=pltpu.SMEM),
            pl.BlockSpec(memory_space=pltpu.VMEM),
        ],
        out_specs=(
            pl.BlockSpec(memory_space=pltpu.VMEM),
            pl.BlockSpec(memory_space=pltpu.VMEM),
            pl.BlockSpec(memory_space=pl.ANY),
        ),
        scratch_shapes=[
            vmem((3, 4, UNIT, D), BF16),
            vmem((2, SHARD, D), BF16),
            vmem((D, CHIP), BF16),
            vmem((CHIP, QUERIES), F32),
            vmem((3, CHIP, QUERIES), BF16),
            vmem((NB, D, BATCH), F32),
            vmem((NB, D, BATCH), F32),
            vmem((NB, 2, D, UNIT), BF16),
            vmem((NB, 2, D, UNIT), BF16),
            vmem((NB, 2, D, UNIT), BF16),
            vmem((NB, 2, D, UNIT), BF16),
            vmem((NB, 2, D, UNIT), BF16),
            vmem((3, D, UNIT), BF16),
            vmem((D, UNIT), F32),
            vmem((SHARD, D), BF16),
            vmem((SHARD, D), BF16),
            vmem((SHARD, D), F32),
            vmem((SHARD, D), BF16),
            vmem((NB, 8, BATCH), F32),
            vmem((NB, 3, 8, BATCH), F32),
            vmem((NB, 8, BATCH), F32),
            vmem((NB, 8, BATCH), F32),
            vmem((NB, 3, 8, BATCH), F32),
            vmem((NB, 8, BATCH), F32),
            vmem((8, UNIT), F32),
            vmem((8, UNIT), F32),
            dma((2 * NB + 1,)), dma((4,)), dma((3,)), dma((3,)),
            dma((NB, PIECES)), dma((NB, PIECES)), dma((NB, PIECES)), dma((NB, PIECES)),
            dma((NB, 2, PIECES)), dma((NB, 2, PIECES)),
            dma((NB, 3)), dma((NB, 3)), dma((NB, 3)), dma((NB, 3)), dma((NB,)), dma((NB,)),
            dma((NB, 4)), dma((NB, 4)), dma((NB, 4)), dma((NB, 4)),
            dma((NB, 4)), dma((3, 2)),
        ],
        compiler_params=pltpu.CompilerParams(
            collective_id=0, has_side_effects=True, vmem_limit_bytes=60 * 1024 * 1024
        ),
        cost_estimate=pl.CostEstimate(
            flops=9 * 2 * 1024**3, bytes_accessed=7 * 2**20, transcendentals=3 * 2**20
        ),
    )(
        queries.reshape(4, 2, UNIT, D),
        passages,
        block_mask,
        positives.reshape(8, UNIT),
    )
    loss, query_grad, passage_grad = pl.pallas_call(
        finish,
        out_shape=(
            jax.ShapeDtypeStruct((8, 128), F32),
            jax.ShapeDtypeStruct((UNIT, D), BF16),
            jax.ShapeDtypeStruct((SHARD, D), BF16),
        ),
        in_specs=[pl.BlockSpec(memory_space=pl.ANY)] * 3,
        out_specs=(pl.BlockSpec(memory_space=pl.ANY),) * 3,
        scratch_shapes=[dma((6,))],
    )(loss, query_grad, passage_grad)
    return loss.reshape(1024), query_grad, passage_grad


def solution(mesh):
    in_specs = (P("qgrp", None), P(("qgrp", "pcol"), None), P(), P("qgrp"))
    out_specs = (P("qgrp"), P(("qgrp", "pcol"), None), P(("qgrp", "pcol"), None))
    return jax.shard_map(
        on_device, mesh=mesh, in_specs=in_specs, out_specs=out_specs, check_vma=False
    )
```

```python
import functools

import jax
import jax.numpy as jnp
from jax import lax
from jax.experimental import pallas as pl
from jax.experimental.pallas import tpu as pltpu
from jax.sharding import PartitionSpec as P

F32 = jnp.float32
BF16 = jnp.bfloat16
D = 1024
SHARD = 1024
CHIP = 2048
UNIT = 128
BATCH = 256
QUERIES = 512
NB = 2
PIECES = 4
HALF = 512
LOW = -1e30
MESH = pl.DeviceIdType.MESH


def dot_nt(a, b):
    return lax.dot_general(a, b, (((1,), (1,)), ((), ())), preferred_element_type=F32)


def dot_nn(a, b):
    return jnp.dot(a, b, preferred_element_type=F32)


def kernel(
    q_hbm, p_hbm, mask_ref, pos_ref,
    loss_ref, qg_ref, pg_ref,
    qv, pv, pt, lg, ev, t1, t0,
    sb, rb, sa, ra, sy, ry, acc,
    pgs, pgr, pgo,
    st, sty, stm, stc, stx, sc, ls, lr,
    load_sem, pair_send, pair_recv,
    qa_send, qa_recv, qb_send, qb_recv, qy_send, qy_recv,
    sty_send, sty_recv, stx_send, stx_recv, stm_send, stm_recv,
    tb_send, tb_recv, ta_send, ta_recv, ty_send, ty_recv,
):
    g = lax.axis_index("qgrp")
    k = lax.axis_index("pcol")
    x = lax.rem(g, 4)
    y = lax.div(k, 2)
    c = lax.rem(k, 2)
    h = lax.rem(y, 2)
    g1 = g + 1 - 2 * lax.rem(x, 2)
    g2 = g + 2 - 4 * lax.div(x, 2)
    g3 = g + 3 - 2 * x
    up = (g, lax.rem(k + 2, 8))
    far = (g, lax.rem(k + 4, 8))
    down = (g, lax.rem(k + 6, 8))
    pair = (g, k + 1 - 2 * c)
    n1, n2, n3 = (g1, k), (g2, k), (g3, k)

    def rcopy(src, dst, ssem, rsem, dev):
        return pltpu.make_async_remote_copy(
            src_ref=src, dst_ref=dst, send_sem=ssem, recv_sem=rsem,
            device_id=dev, device_id_type=MESH,
        )

    loads = [pltpu.make_async_copy(p_hbm, pv.at[0], load_sem.at[NB * 2])]
    for b in range(NB):
        for j in range(2):
            slot = 2 * b + j
            loads.append(
                pltpu.make_async_copy(q_hbm.at[b + 2 * j, c], qv.at[0, slot], load_sem.at[slot])
            )
    for copy in loads:
        copy.start()

    barrier = pltpu.get_barrier_semaphore()
    for dev in (up, far, down, pair, n1, n2, n3):
        pl.semaphore_signal(barrier, inc=1, device_id=dev, device_id_type=MESH)
    pl.semaphore_wait(barrier, 7)

    p_swap = rcopy(p_hbm, pv.at[1], pair_send.at[0], pair_recv.at[0], pair)
    sends = [p_swap]

    def start(copy):
        copy.start()
        sends.append(copy)

    def rows(i):
        return pl.ds(64 * (i % 2) + 32 * (i // 2), 32)

    def qa(b, i):
        return rcopy(
            q_hbm.at[b + 2 * h, c, rows(i)], qv.at[1, 2 * b + h, rows(i)],
            qa_send.at[b, i], qa_recv.at[b, i], n1,
        )

    def qb(b, i):
        return rcopy(
            qv.at[1, 2 * b + h, rows(i)], qv.at[2, 2 * b + h, rows(i)],
            qb_send.at[b, i], qb_recv.at[b, i], n3,
        )

    def qy(b, r, i):
        block = qv.at[1 + r, 2 * b + h, rows(i)]
        return rcopy(
            block, block, qy_send.at[b, r, i], qy_recv.at[b, r, i], (up, down)[i % 2]
        )

    def qy_wait(b, r):
        for i in range(PIECES):
            block = qv.at[1 + r, 2 * b + 1 - h, rows(i)]
            rcopy(
                block, block, qy_send.at[b, r, i], qy_recv.at[b, r, i], (up, down)[i % 2]
            ).wait_recv()

    for b in range(NB):
        for i in range(PIECES):
            start(qa(b, i))
    p_swap.start()

    def forward_a(b, i):
        qa(b, i).wait_recv()
        start(qb(b, i))
        start(qy(b, 0, i))

    def forward_b(b, i):
        qb(b, i).wait_recv()
        start(qy(b, 1, i))

    flags = [mask_ref[0, g1] > 0, mask_ref[1, g2] > 0]

    def positive_row(b):
        return jnp.concatenate(
            [pos_ref[pl.ds(2 * (b + 2 * j) + c, 1), :] for j in range(2)], axis=1
        )

    def first_column(half):
        return (k if half == 0 else k + 1 - 2 * c) * SHARD

    ls[...] = jnp.zeros((8, UNIT), F32)
    for copy in loads:
        copy.wait()
    own_max = jnp.full((1, QUERIES), LOW, F32)

    def own_logits(half, peak):
        def body(i, peak):
            own_queries = qv[0].reshape(QUERIES, D)
            block = dot_nt(pv[half, pl.ds(i * 512, 512), :], own_queries)
            lg[pl.ds(half * SHARD + i * 512, 512), :] = block
            return jnp.maximum(peak, jnp.max(block, axis=0, keepdims=True))

        return lax.fori_loop(0, 2, body, peak)

    def transpose(half):
        for i in range(4):
            first = half * SHARD + i * 256
            pt[:, first:first + 256] = pv[half, pl.ds(i * 256, 256), :].T

    own_max = own_logits(0, own_max)
    transpose(0)
    forward_a(0, 0)
    forward_a(0, 1)
    p_swap.wait_recv()
    own_max = own_logits(1, own_max)
    forward_a(0, 2)
    forward_b(0, 0)
    forward_a(0, 3)
    forward_b(0, 1)
    transpose(1)
    forward_a(1, 0)
    forward_b(0, 2)

    positive_all = jnp.concatenate([positive_row(b) for b in range(NB)], axis=1)

    def own_exp(half, carry):
        def body(i, carry):
            total, positive = carry
            r = half * SHARD + i * 256
            block = lg[pl.ds(r, 256), :]
            column = lax.broadcasted_iota(jnp.int32, (256, QUERIES), 0) + (
                first_column(half) + i * 256
            )
            e = jnp.exp(block - own_max)
            ev[0, pl.ds(r, 256), :] = e.astype(BF16)
            total = total + jnp.sum(e, axis=0, keepdims=True)
            positive = positive + jnp.sum(
                jnp.where(column == positive_all, block, 0.0), axis=0, keepdims=True
            )
            return total, positive

        return lax.fori_loop(0, 4, body, carry)

    zero = jnp.zeros((1, QUERIES), F32)
    own_sums = own_exp(0, (zero, zero))
    forward_a(1, 1)
    forward_b(0, 3)
    own_total, own_positive = own_exp(1, own_sums)
    for b in range(NB):
        part = slice(b * BATCH, (b + 1) * BATCH)
        st[b, 0:1, :] = own_max[:, part]
        st[b, 3:4, :] = own_total[:, part]
        st[b, 6:7, :] = own_positive[:, part]
        st[b, 7:8, :] = jnp.zeros((1, BATCH), F32)

    def lent(b, r):
        def body(half, peak):
            queries = qv[1 + r, 2 * b:2 * b + 2].reshape(BATCH, D)
            block = dot_nt(pv[half], queries)
            lg[pl.ds(half * SHARD, SHARD), 0:BATCH] = block
            return jnp.maximum(peak, jnp.max(block, axis=0, keepdims=True))

        peak = lax.fori_loop(0, 2, body, jnp.full((1, BATCH), LOW, F32))

        def exp_body(i, total):
            e = jnp.exp(lg[pl.ds(i * 256, 256), 0:BATCH] - peak)
            ev[1 + r, pl.ds(i * 256, 256), b * BATCH:(b + 1) * BATCH] = e.astype(BF16)
            return total + jnp.sum(e, axis=0, keepdims=True)

        total = lax.fori_loop(0, 8, exp_body, jnp.zeros((1, BATCH), F32))
        st[b, 1 + r:2 + r, :] = jnp.where(flags[r], peak, LOW)
        st[b, 4 + r:5 + r, :] = total

    def stats_y(b, i):
        dev = (down, far, up)[i]
        return rcopy(st.at[b], sty.at[b, i], sty_send.at[b, i], sty_recv.at[b, i], dev)

    def stats_m(b):
        return rcopy(st.at[b], stm.at[b], stm_send.at[b], stm_recv.at[b], n3)

    def stats_x(b, i):
        dev = (n1, n2, n3)[i]
        return rcopy(stc.at[b], stx.at[b, i], stx_send.at[b, i], stx_recv.at[b, i], dev)

    def combine_y(b):
        for i in range(3):
            stats_y(b, i).wait_recv()
        peaks = [st[b, 0:3, :]] + [sty[b, i, 0:3, :] for i in range(3)]
        sums = [st[b, 3:6, :]] + [sty[b, i, 3:6, :] for i in range(3)]
        peak = functools.reduce(jnp.maximum, peaks)
        total = sum(s * jnp.exp(m - peak) for s, m in zip(sums, peaks))
        positive = st[b, 6:7, :] + sty[b, 0, 6:7, :] + sty[b, 1, 6:7, :] + sty[b, 2, 6:7, :]
        stc[b, 0:3, :] = peak
        stc[b, 3:6, :] = total
        stc[b, 6:7, :] = positive
        stc[b, 7:8, :] = jnp.zeros((1, BATCH), F32)

    def combine_x(b):
        for i in range(3):
            stats_x(b, i).wait_recv()
        own, one, two, three = stc[b], stx[b, 0], stx[b, 1], stx[b, 2]
        sources = (
            ((own, 0), (one, 1), (two, 2)),
            ((one, 0), (own, 1), (three, 2)),
            ((two, 0), (own, 2), (three, 1)),
        )
        log_totals = []
        for source in sources:
            peaks = [a[r:r + 1] for a, r in source]
            sums = [a[3 + r:4 + r] for a, r in source]
            peak = functools.reduce(jnp.maximum, peaks)
            total = sum(s * jnp.exp(m - peak) for s, m in zip(sums, peaks))
            log_totals.append(peak + jnp.log(total))
        for r in range(3):
            sc[b, r:r + 1, :] = jnp.exp(st[b, r:r + 1, :] - log_totals[r])
        stats_m(b).wait_recv()
        sc[b, 4:5, :] = jnp.exp(stm[b, 2:3, :] - log_totals[1])
        positive = own[6:7]
        sc[b, 3:4, :] = jnp.exp(positive - log_totals[0]) - 1.0
        loss = log_totals[0] - positive
        for j in range(2):
            ls[b + 2 * j:b + 2 * j + 1, :] = loss[:, j * UNIT:(j + 1) * UNIT]

    def term(b, r, i):
        return dot_nn(pt[pl.ds(i * HALF, HALF), :], ev[r, :, b * BATCH:(b + 1) * BATCH])

    def terms(b, r):
        target = t0 if r == 0 else t1

        @pl.loop(0, 2)
        def _(i):
            target[b, pl.ds(i * HALF, HALF), :] = term(b, r, i)

    def own_weights(b):
        scale, less = sc[b, 0:1, :], sc[b, 3:4, :]
        where = positive_row(b)
        for half in range(2):
            @pl.loop(0, 4)
            def _(i):
                span = pl.ds(half * SHARD + i * 256, 256)
                column = lax.broadcasted_iota(jnp.int32, (256, BATCH), 0) + (
                    first_column(half) + i * 256
                )
                e = ev[0, span, b * BATCH:(b + 1) * BATCH].astype(F32)
                w = jnp.where(column == where, less, e * scale)
                ev[0, span, b * BATCH:(b + 1) * BATCH] = w.astype(BF16)

    def lent_weights(b, r):
        scale = sc[b, 1 + r:2 + r, :]

        @pl.loop(0, 8)
        def _(i):
            span = pl.ds(i * 256, 256)
            e = ev[1 + r, span, b * BATCH:(b + 1) * BATCH].astype(F32)
            ev[1 + r, span, b * BATCH:(b + 1) * BATCH] = (e * scale).astype(BF16)

    def part(n):
        return n % 2, pl.ds(HALF * (n // 2), HALF)

    def tb(b, n):
        j, d = part(n)
        return rcopy(
            sb.at[b, j, d], rb.at[b, j, d], tb_send.at[b, n], tb_recv.at[b, n], n3
        )

    def ta(b, n):
        j, d = part(n)
        return rcopy(
            sa.at[b, j, d], ra.at[b, j, d], ta_send.at[b, n], ta_recv.at[b, n], n1
        )

    def ty(b, n):
        j, d = part(n)
        unit = b + 2 * j
        slot = lax.rem(y - unit + 4, 4) - 1
        return rcopy(
            sy.at[b, j, d], ry.at[slot, d], ty_send.at[b, n], ty_recv.at[slot, n // 2],
            (g, 2 * unit + c),
        )

    def lanes(j):
        return slice(j * UNIT, (j + 1) * UNIT)

    def send_b(b, i):
        total = term(b, 2, i).astype(BF16)
        for j in range(2):
            sb[b, j, pl.ds(i * HALF, HALF), :] = total[:, lanes(j)]
            start(tb(b, 2 * i + j))

    def send_a(b, n):
        j, d = part(n)
        tb(b, n).wait_recv()
        sa[b, j, d] = (
            t1[b, d, lanes(j)] * sc[b, 1:2, lanes(j)]
            + rb[b, j, d].astype(F32) * sc[b, 4:5, lanes(j)]
        ).astype(BF16)
        start(ta(b, n))

    def send_y(b, n):
        j, d = part(n)
        unit = b + 2 * j
        ta(b, n).wait_recv()

        @pl.when(y == unit)
        def _():
            acc[d] = t0[b, d, lanes(j)] + ra[b, j, d].astype(F32)

        @pl.when(y != unit)
        def _():
            sy[b, j, d] = (t0[b, d, lanes(j)] + ra[b, j, d].astype(F32)).astype(BF16)
            ty(b, n).start()

    def passage_part(half, i, target):
        total = None
        for r in range(3):
            add = dot_nn(
                ev[r, pl.ds(half * SHARD + i * 512, 512), :], qv[r].reshape(QUERIES, D)
            )
            total = add if total is None else total + add
        target[pl.ds(i * 512, 512), :] = total.astype(target.dtype)

    def begin_stats(b):
        start(stats_m(b))
        for i in range(3):
            start(stats_y(b, i))

    def begin_stats_x(b):
        combine_y(b)
        for i in range(3):
            start(stats_x(b, i))

    qy_wait(0, 0)
    lent(0, 0)
    forward_a(1, 2)
    forward_b(1, 0)
    forward_a(1, 3)
    forward_b(1, 1)
    qy_wait(0, 1)
    lent(0, 1)
    begin_stats(0)
    send_b(0, 0)
    forward_b(1, 2)
    send_b(0, 1)
    forward_b(1, 3)
    begin_stats_x(0)
    terms(0, 1)
    qy_wait(1, 0)
    lent(1, 0)
    combine_x(0)
    send_a(0, 0)
    qy_wait(1, 1)
    lent(1, 1)
    begin_stats(1)
    send_a(0, 1)
    send_b(1, 0)
    send_b(1, 1)
    send_a(0, 2)
    own_weights(0)
    terms(0, 0)
    send_a(0, 3)
    begin_stats_x(1)
    send_y(0, 0)
    send_y(0, 1)
    terms(1, 1)
    lent_weights(0, 0)
    lent_weights(0, 1)
    combine_x(1)
    loss_copy = rcopy(ls, lr, pair_send.at[1], pair_recv.at[1], pair)
    start(loss_copy)
    send_y(0, 2)
    send_a(1, 0)
    own_weights(1)
    terms(1, 0)
    send_a(1, 1)
    send_y(0, 3)
    lent_weights(1, 0)
    lent_weights(1, 1)
    passage_part(1, 0, pgs)
    send_a(1, 2)
    passage_part(1, 1, pgs)
    pg_copy = rcopy(pgs, pgr, pair_send.at[2], pair_recv.at[2], pair)
    start(pg_copy)
    send_a(1, 3)
    send_y(1, 0)
    passage_part(0, 0, pgo)
    send_y(1, 1)
    passage_part(0, 1, pgo)
    send_y(1, 2)
    send_y(1, 3)
    loss_copy.wait_recv()
    for j in range(4):
        loss_ref[pl.ds(2 * j + c, 1), :] = ls[j:j + 1, :]
        loss_ref[pl.ds(2 * j + 1 - c, 1), :] = lr[j:j + 1, :]
    pg_copy.wait_recv()
    for i in range(4):
        span = pl.ds(i * 256, 256)
        pg_ref[span, :] = (pgo[span, :] + pgr[span, :].astype(F32)).astype(BF16)
    for i in range(2):
        d = slice(i * HALF, (i + 1) * HALF)
        total = acc[d]
        for slot in range(3):
            rcopy(
                sy.at[0, 0, d], ry.at[slot, d], ty_send.at[0, 0], ty_recv.at[slot, i], up
            ).wait_recv()
            total = total + ry[slot, d].astype(F32)
        qg_ref[:, d] = total.T.astype(BF16)
    for copy in sends:
        copy.wait_send()
    for b in range(NB):
        for n in range(4):
            @pl.when(y != b + 2 * (n % 2))
            def _():
                ty(b, n).wait_send()


def on_device(queries, passages, block_mask, positives):
    vmem = pltpu.VMEM
    dma = pltpu.SemaphoreType.DMA
    loss, query_grad, passage_grad = pl.pallas_call(
        kernel,
        out_shape=(
            pltpu.VMEM((8, 128), F32),
            pltpu.VMEM((UNIT, D), BF16),
            pltpu.VMEM((SHARD, D), BF16),
        ),
        in_specs=[
            pl.BlockSpec(memory_space=pl.ANY),
            pl.BlockSpec(memory_space=pl.ANY),
            pl.BlockSpec(memory_space=pltpu.SMEM),
            pl.BlockSpec(memory_space=pltpu.VMEM),
        ],
        out_specs=(
            pl.BlockSpec(memory_space=pltpu.VMEM),
            pl.BlockSpec(memory_space=pltpu.VMEM),
            pl.BlockSpec(memory_space=pltpu.VMEM),
        ),
        scratch_shapes=[
            vmem((3, 4, UNIT, D), BF16),
            vmem((2, SHARD, D), BF16),
            vmem((D, CHIP), BF16),
            vmem((CHIP, QUERIES), F32),
            vmem((3, CHIP, QUERIES), BF16),
            vmem((NB, D, BATCH), F32),
            vmem((NB, D, BATCH), F32),
            vmem((NB, 2, D, UNIT), BF16),
            vmem((NB, 2, D, UNIT), BF16),
            vmem((NB, 2, D, UNIT), BF16),
            vmem((NB, 2, D, UNIT), BF16),
            vmem((NB, 2, D, UNIT), BF16),
            vmem((3, D, UNIT), BF16),
            vmem((D, UNIT), F32),
            vmem((SHARD, D), BF16),
            vmem((SHARD, D), BF16),
            vmem((SHARD, D), F32),
            vmem((NB, 8, BATCH), F32),
            vmem((NB, 3, 8, BATCH), F32),
            vmem((NB, 8, BATCH), F32),
            vmem((NB, 8, BATCH), F32),
            vmem((NB, 3, 8, BATCH), F32),
            vmem((NB, 8, BATCH), F32),
            vmem((8, UNIT), F32),
            vmem((8, UNIT), F32),
            dma((2 * NB + 1,)), dma((3,)), dma((3,)),
            dma((NB, PIECES)), dma((NB, PIECES)), dma((NB, PIECES)), dma((NB, PIECES)),
            dma((NB, 2, PIECES)), dma((NB, 2, PIECES)),
            dma((NB, 3)), dma((NB, 3)), dma((NB, 3)), dma((NB, 3)), dma((NB,)), dma((NB,)),
            dma((NB, 4)), dma((NB, 4)), dma((NB, 4)), dma((NB, 4)),
            dma((NB, 4)), dma((3, 2)),
        ],
        compiler_params=pltpu.CompilerParams(
            collective_id=0, has_side_effects=True, vmem_limit_bytes=52 * 1024 * 1024
        ),
        cost_estimate=pl.CostEstimate(
            flops=9 * 2 * 1024**3, bytes_accessed=7 * 2**20, transcendentals=3 * 2**20
        ),
    )(
        queries.reshape(4, 2, UNIT, D),
        passages,
        block_mask,
        positives.reshape(8, UNIT),
    )
    return loss.reshape(1024), query_grad, passage_grad


def solution(mesh):
    in_specs = (P("qgrp", None), P(("qgrp", "pcol"), None), P(), P("qgrp"))
    out_specs = (P("qgrp"), P(("qgrp", "pcol"), None), P(("qgrp", "pcol"), None))
    return jax.shard_map(
        on_device, mesh=mesh, in_specs=in_specs, out_specs=out_specs, check_vma=False
    )
```

```python
import functools

import jax
import jax.numpy as jnp
from jax import lax
from jax.experimental import pallas as pl
from jax.experimental.pallas import tpu as pltpu
from jax.sharding import PartitionSpec as P

F32 = jnp.float32
BF16 = jnp.bfloat16
D = 1024
SHARD = 1024
CHIP = 2048
UNIT = 128
BATCH = 256
QUERIES = 512
NB = 2
PIECES = 4
HALF = 512
PARTS = 4
PART = 256
ROWS = 256
LOW = -1e30
MESH = pl.DeviceIdType.MESH


def dot_nt(a, b):
    return lax.dot_general(a, b, (((1,), (1,)), ((), ())), preferred_element_type=F32)


def dot_nn(a, b):
    return jnp.dot(a, b, preferred_element_type=F32)


def kernel(
    q_hbm, p_hbm, mask_ref, pos_ref,
    loss_ref, qg_ref, pg_ref,
    qv, pv, pt, lg, ev, t1, t0,
    sb, rb, sa, ra, sy, ry, acc,
    pgs, pgr, pgo,
    st, sty, stm, stc, stx, sc, sd, pas, par, ls, lr,
    load_sem, pair_send, pair_recv,
    qa_send, qa_recv, qb_send, qb_recv, qy_send, qy_recv,
    sty_send, sty_recv, stx_send, stx_recv, stm_send, stm_recv, pa_send, pa_recv,
    tb_send, tb_recv, ta_send, ta_recv, ty_send, ty_recv,
):
    g = lax.axis_index("qgrp")
    k = lax.axis_index("pcol")
    x = lax.rem(g, 4)
    y = lax.div(k, 2)
    c = lax.rem(k, 2)
    h = lax.rem(y, 2)
    g1 = g + 1 - 2 * lax.rem(x, 2)
    g2 = g + 2 - 4 * lax.div(x, 2)
    g3 = g + 3 - 2 * x
    up = (g, lax.rem(k + 2, 8))
    far = (g, lax.rem(k + 4, 8))
    down = (g, lax.rem(k + 6, 8))
    pair = (g, k + 1 - 2 * c)
    n1, n2, n3 = (g1, k), (g2, k), (g3, k)

    def rcopy(src, dst, ssem, rsem, dev):
        return pltpu.make_async_remote_copy(
            src_ref=src, dst_ref=dst, send_sem=ssem, recv_sem=rsem,
            device_id=dev, device_id_type=MESH,
        )

    loads = [pltpu.make_async_copy(p_hbm, pv.at[0], load_sem.at[NB * 2])]
    for b in range(NB):
        for j in range(2):
            slot = 2 * b + j
            loads.append(
                pltpu.make_async_copy(q_hbm.at[b + 2 * j, c], qv.at[0, slot], load_sem.at[slot])
            )
    for copy in loads:
        copy.start()

    barrier = pltpu.get_barrier_semaphore()
    for dev in (up, far, down, pair, n1, n2, n3):
        pl.semaphore_signal(barrier, inc=1, device_id=dev, device_id_type=MESH)
    pl.semaphore_wait(barrier, 7)

    p_swap = rcopy(p_hbm, pv.at[1], pair_send.at[0], pair_recv.at[0], pair)
    sends = [p_swap]

    def start(copy):
        copy.start()
        sends.append(copy)

    def rows(i):
        return pl.ds(64 * (i % 2) + 32 * (i // 2), 32)

    def qa(b, i):
        return rcopy(
            q_hbm.at[b + 2 * h, c, rows(i)], qv.at[1, 2 * b + h, rows(i)],
            qa_send.at[b, i], qa_recv.at[b, i], n1,
        )

    def qb(b, i):
        return rcopy(
            qv.at[1, 2 * b + h, rows(i)], qv.at[2, 2 * b + h, rows(i)],
            qb_send.at[b, i], qb_recv.at[b, i], n3,
        )

    def qy(b, r, i):
        block = qv.at[1 + r, 2 * b + h, rows(i)]
        return rcopy(
            block, block, qy_send.at[b, r, i], qy_recv.at[b, r, i], (up, down)[i % 2]
        )

    def qy_wait(b, r):
        for i in range(PIECES):
            block = qv.at[1 + r, 2 * b + 1 - h, rows(i)]
            rcopy(
                block, block, qy_send.at[b, r, i], qy_recv.at[b, r, i], (up, down)[i % 2]
            ).wait_recv()

    for b in range(NB):
        for i in range(PIECES):
            start(qa(b, i))
    p_swap.start()

    def forward_a(b, i):
        qa(b, i).wait_recv()
        start(qb(b, i))
        start(qy(b, 0, i))

    def forward_b(b, i):
        qb(b, i).wait_recv()
        start(qy(b, 1, i))

    flags = [mask_ref[0, g1] > 0, mask_ref[1, g2] > 0]

    def positive_row(b):
        return jnp.concatenate(
            [pos_ref[pl.ds(2 * (b + 2 * j) + c, 1), :] for j in range(2)], axis=1
        )

    def first_column(half):
        return (k if half == 0 else k + 1 - 2 * c) * SHARD

    ls[...] = jnp.zeros((8, UNIT), F32)
    for copy in loads:
        copy.wait()
    own_max = jnp.full((1, QUERIES), LOW, F32)

    def own_logits(half, peak):
        def body(i, peak):
            own_queries = qv[0].reshape(QUERIES, D)
            block = dot_nt(pv[half, pl.ds(i * 512, 512), :], own_queries)
            lg[pl.ds(half * SHARD + i * 512, 512), :] = block
            return jnp.maximum(peak, jnp.max(block, axis=0, keepdims=True))

        return lax.fori_loop(0, 2, body, peak)

    def transpose(half):
        for i in range(4):
            first = half * SHARD + i * 256
            pt[:, first:first + 256] = pv[half, pl.ds(i * 256, 256), :].T

    own_max = own_logits(0, own_max)
    transpose(0)
    forward_a(0, 0)
    forward_a(0, 1)
    p_swap.wait_recv()
    own_max = own_logits(1, own_max)
    forward_a(0, 2)
    forward_b(0, 0)
    forward_a(0, 3)
    forward_b(0, 1)
    transpose(1)
    forward_a(1, 0)
    forward_b(0, 2)

    positive_all = jnp.concatenate([positive_row(b) for b in range(NB)], axis=1)

    def own_exp(half, carry):
        def body(i, carry):
            total, positive = carry
            r = half * SHARD + i * 256
            block = lg[pl.ds(r, 256), :]
            column = lax.broadcasted_iota(jnp.int32, (256, QUERIES), 0) + (
                first_column(half) + i * 256
            )
            e = jnp.exp(block - own_max)
            ev[0, pl.ds(r, 256), :] = e.astype(BF16)
            total = total + jnp.sum(e, axis=0, keepdims=True)
            positive = positive + jnp.sum(
                jnp.where(column == positive_all, block, 0.0), axis=0, keepdims=True
            )
            return total, positive

        return lax.fori_loop(0, 4, body, carry)

    zero = jnp.zeros((1, QUERIES), F32)
    own_sums = own_exp(0, (zero, zero))
    forward_a(1, 1)
    forward_b(0, 3)
    own_total, own_positive = own_exp(1, own_sums)
    for b in range(NB):
        part = slice(b * BATCH, (b + 1) * BATCH)
        st[b, 0:1, :] = own_max[:, part]
        st[b, 3:4, :] = own_total[:, part]
        st[b, 6:7, :] = own_positive[:, part]
        st[b, 7:8, :] = jnp.zeros((1, BATCH), F32)

    def lent(b, r):
        def body(half, peak):
            queries = qv[1 + r, 2 * b:2 * b + 2].reshape(BATCH, D)
            block = dot_nt(pv[half], queries)
            lg[pl.ds(half * SHARD, SHARD), 0:BATCH] = block
            return jnp.maximum(peak, jnp.max(block, axis=0, keepdims=True))

        peak = lax.fori_loop(0, 2, body, jnp.full((1, BATCH), LOW, F32))

        def exp_body(i, total):
            e = jnp.exp(lg[pl.ds(i * 256, 256), 0:BATCH] - peak)
            ev[1 + r, pl.ds(i * 256, 256), b * BATCH:(b + 1) * BATCH] = e.astype(BF16)
            return total + jnp.sum(e, axis=0, keepdims=True)

        total = lax.fori_loop(0, 8, exp_body, jnp.zeros((1, BATCH), F32))
        st[b, 1 + r:2 + r, :] = jnp.where(flags[r], peak, LOW)
        st[b, 4 + r:5 + r, :] = total

    def stats_y(b, i):
        dev = (down, far, up)[i]
        return rcopy(st.at[b], sty.at[b, i], sty_send.at[b, i], sty_recv.at[b, i], dev)

    def stats_m(b):
        return rcopy(st.at[b], stm.at[b], stm_send.at[b], stm_recv.at[b], n3)

    def peak_a(b):
        return rcopy(pas.at[b], par.at[b], pa_send.at[b], pa_recv.at[b], n1)

    def pair_scale(b):
        stats_m(b).wait_recv()
        here, there = st[b, 1:2, :], stm[b, 2:3, :]
        peak = jnp.maximum(here, there)
        sd[b, 0:1, :] = jnp.exp(here - peak)
        sd[b, 1:2, :] = jnp.exp(there - peak)
        pas[b] = jnp.broadcast_to(peak, (8, BATCH))
        start(peak_a(b))

    def stats_x(b, i):
        dev = (n1, n2, n3)[i]
        return rcopy(stc.at[b], stx.at[b, i], stx_send.at[b, i], stx_recv.at[b, i], dev)

    def combine_y(b):
        for i in range(3):
            stats_y(b, i).wait_recv()
        peaks = [st[b, 0:3, :]] + [sty[b, i, 0:3, :] for i in range(3)]
        sums = [st[b, 3:6, :]] + [sty[b, i, 3:6, :] for i in range(3)]
        peak = functools.reduce(jnp.maximum, peaks)
        total = sum(s * jnp.exp(m - peak) for s, m in zip(sums, peaks))
        positive = st[b, 6:7, :] + sty[b, 0, 6:7, :] + sty[b, 1, 6:7, :] + sty[b, 2, 6:7, :]
        stc[b, 0:3, :] = peak
        stc[b, 3:6, :] = total
        stc[b, 6:7, :] = positive
        stc[b, 7:8, :] = jnp.zeros((1, BATCH), F32)

    def combine_x(b):
        for i in range(3):
            stats_x(b, i).wait_recv()
        own, one, two, three = stc[b], stx[b, 0], stx[b, 1], stx[b, 2]
        sources = (
            ((own, 0), (one, 1), (two, 2)),
            ((one, 0), (own, 1), (three, 2)),
            ((two, 0), (own, 2), (three, 1)),
        )
        log_totals = []
        for source in sources:
            peaks = [a[r:r + 1] for a, r in source]
            sums = [a[3 + r:4 + r] for a, r in source]
            peak = functools.reduce(jnp.maximum, peaks)
            total = sum(s * jnp.exp(m - peak) for s, m in zip(sums, peaks))
            log_totals.append(peak + jnp.log(total))
        for r in range(3):
            sc[b, r:r + 1, :] = jnp.exp(st[b, r:r + 1, :] - log_totals[r])
        peak_a(b).wait_recv()
        sc[b, 4:5, :] = jnp.exp(par[b, 0:1, :] - log_totals[0])
        positive = own[6:7]
        sc[b, 3:4, :] = jnp.exp(positive - log_totals[0]) - 1.0
        loss = log_totals[0] - positive
        for j in range(2):
            ls[b + 2 * j:b + 2 * j + 1, :] = loss[:, j * UNIT:(j + 1) * UNIT]

    def term(b, r, i):
        return dot_nn(pt[pl.ds(i * HALF, HALF), :], ev[r, :, b * BATCH:(b + 1) * BATCH])

    def terms(b, r):
        target = t0 if r == 0 else t1

        @pl.loop(0, 2)
        def _(i):
            target[b, pl.ds(i * HALF, HALF), :] = term(b, r, i)

    def own_weights(b):
        scale, less = sc[b, 0:1, :], sc[b, 3:4, :]
        where = positive_row(b)
        for half in range(2):
            @pl.loop(0, 4)
            def _(i):
                span = pl.ds(half * SHARD + i * 256, 256)
                column = lax.broadcasted_iota(jnp.int32, (256, BATCH), 0) + (
                    first_column(half) + i * 256
                )
                e = ev[0, span, b * BATCH:(b + 1) * BATCH].astype(F32)
                w = jnp.where(column == where, less, e * scale)
                ev[0, span, b * BATCH:(b + 1) * BATCH] = w.astype(BF16)

    def lent_weights(b, r):
        scale = sc[b, 1 + r:2 + r, :]

        @pl.loop(0, 8)
        def _(i):
            span = pl.ds(i * 256, 256)
            e = ev[1 + r, span, b * BATCH:(b + 1) * BATCH].astype(F32)
            ev[1 + r, span, b * BATCH:(b + 1) * BATCH] = (e * scale).astype(BF16)

    def part(n):
        return n % 2, pl.ds(PART * (n // 2), PART)

    def tb(b, n):
        j, d = part(n)
        return rcopy(
            sb.at[b, j, d], rb.at[b, j, d], tb_send.at[b, n], tb_recv.at[b, n], n3
        )

    def ta(b, n):
        j, d = part(n)
        return rcopy(
            sa.at[b, j, d], ra.at[b, j, d], ta_send.at[b, n], ta_recv.at[b, n], n1
        )

    def ty(b, n):
        j, d = part(n)
        unit = b + 2 * j
        slot = lax.rem(y - unit + 4, 4) - 1
        return rcopy(
            sy.at[b, j, d], ry.at[slot, d], ty_send.at[b, n], ty_recv.at[slot, n // 2],
            (g, 2 * unit + c),
        )

    def lanes(j):
        return slice(j * UNIT, (j + 1) * UNIT)

    def send_b(b, i):
        total = term(b, 2, i).astype(BF16)
        for j in range(2):
            sb[b, j, pl.ds(i * HALF, HALF), :] = total[:, lanes(j)]
        for n in range(PARTS):
            start(tb(b, PARTS * i + n))

    def send_a(b, n):
        j, d = part(n)
        tb(b, n).wait_recv()
        sa[b, j, d] = (
            t1[b, d, lanes(j)] * sd[b, 0:1, lanes(j)]
            + rb[b, j, d].astype(F32) * sd[b, 1:2, lanes(j)]
        ).astype(BF16)
        start(ta(b, n))

    def send_y(b, n):
        j, d = part(n)
        unit = b + 2 * j
        ta(b, n).wait_recv()
        total = t0[b, d, lanes(j)] + ra[b, j, d].astype(F32) * sc[b, 4:5, lanes(j)]

        @pl.when(y == unit)
        def _():
            acc[d] = total

        @pl.when(y != unit)
        def _():
            sy[b, j, d] = total.astype(BF16)
            ty(b, n).start()

    def passage_part(half, i, target):
        total = None
        for r in range(3):
            add = dot_nn(
                ev[r, pl.ds(half * SHARD + i * ROWS, ROWS), :], qv[r].reshape(QUERIES, D)
            )
            total = add if total is None else total + add
        target[pl.ds(i * ROWS, ROWS), :] = total.astype(target.dtype)

    def begin_stats(b):
        start(stats_m(b))
        for i in range(3):
            start(stats_y(b, i))

    def begin_stats_x(b):
        combine_y(b)
        for i in range(3):
            start(stats_x(b, i))

    def send_a_all(b, *pieces):
        for n in pieces:
            send_a(b, n)

    def send_y_all(b, *pieces):
        for n in pieces:
            send_y(b, n)

    qy_wait(0, 0)
    lent(0, 0)
    forward_a(1, 2)
    forward_b(1, 0)
    forward_a(1, 3)
    forward_b(1, 1)
    qy_wait(0, 1)
    lent(0, 1)
    begin_stats(0)
    send_b(0, 0)
    forward_b(1, 2)
    send_b(0, 1)
    forward_b(1, 3)
    terms(0, 1)
    begin_stats_x(0)
    pair_scale(0)
    qy_wait(1, 0)
    lent(1, 0)
    send_a_all(0, 0, 1)
    qy_wait(1, 1)
    lent(1, 1)
    begin_stats(1)
    send_a_all(0, 2)
    send_b(1, 0)
    send_b(1, 1)
    send_a_all(0, 3, 4)
    combine_x(0)
    own_weights(0)
    terms(0, 0)
    send_a_all(0, 5, 6)
    send_y_all(0, 0, 1, 2)
    terms(1, 1)
    send_a_all(0, 7)
    send_y_all(0, 3, 4)
    begin_stats_x(1)
    pair_scale(1)
    lent_weights(0, 0)
    lent_weights(0, 1)
    send_a_all(1, 0)
    send_y_all(0, 5)
    send_a_all(1, 1)
    send_y_all(0, 6)
    send_a_all(1, 2)
    send_y_all(0, 7)
    combine_x(1)
    loss_copy = rcopy(ls, lr, pair_send.at[1], pair_recv.at[1], pair)
    start(loss_copy)
    own_weights(1)
    terms(1, 0)
    send_a_all(1, 3, 4)
    send_y_all(1, 0, 1)
    lent_weights(1, 0)
    lent_weights(1, 1)
    passage_part(1, 0, pgs)
    passage_part(1, 1, pgs)
    send_a_all(1, 5)
    send_y_all(1, 2)
    send_a_all(1, 6)
    send_y_all(1, 3)
    passage_part(1, 2, pgs)
    send_a_all(1, 7)
    send_y_all(1, 4)
    passage_part(1, 3, pgs)
    pg_copy = rcopy(pgs, pgr, pair_send.at[2], pair_recv.at[2], pair)
    start(pg_copy)
    send_y_all(1, 5)
    passage_part(0, 0, pgo)
    send_y_all(1, 6)
    passage_part(0, 1, pgo)
    send_y_all(1, 7)
    passage_part(0, 2, pgo)
    passage_part(0, 3, pgo)
    loss_copy.wait_recv()
    for j in range(4):
        loss_ref[pl.ds(2 * j + c, 1), :] = ls[j:j + 1, :]
        loss_ref[pl.ds(2 * j + 1 - c, 1), :] = lr[j:j + 1, :]
    pg_copy.wait_recv()
    for i in range(4):
        span = pl.ds(i * 256, 256)
        pg_ref[span, :] = (pgo[span, :] + pgr[span, :].astype(F32)).astype(BF16)
    for i in range(PARTS):
        d = slice(i * PART, (i + 1) * PART)
        total = acc[d]
        for slot in range(3):
            rcopy(
                sy.at[0, 0, d], ry.at[slot, d], ty_send.at[0, 0], ty_recv.at[slot, i], up
            ).wait_recv()
            total = total + ry[slot, d].astype(F32)
        qg_ref[:, d] = total.T.astype(BF16)
    for copy in sends:
        copy.wait_send()
    for b in range(NB):
        for n in range(2 * PARTS):
            @pl.when(y != b + 2 * (n % 2))
            def _():
                ty(b, n).wait_send()


def on_device(queries, passages, block_mask, positives):
    vmem = pltpu.VMEM
    dma = pltpu.SemaphoreType.DMA
    loss, query_grad, passage_grad = pl.pallas_call(
        kernel,
        out_shape=(
            pltpu.VMEM((8, 128), F32),
            pltpu.VMEM((UNIT, D), BF16),
            pltpu.VMEM((SHARD, D), BF16),
        ),
        in_specs=[
            pl.BlockSpec(memory_space=pl.ANY),
            pl.BlockSpec(memory_space=pl.ANY),
            pl.BlockSpec(memory_space=pltpu.SMEM),
            pl.BlockSpec(memory_space=pltpu.VMEM),
        ],
        out_specs=(
            pl.BlockSpec(memory_space=pltpu.VMEM),
            pl.BlockSpec(memory_space=pltpu.VMEM),
            pl.BlockSpec(memory_space=pltpu.VMEM),
        ),
        scratch_shapes=[
            vmem((3, 4, UNIT, D), BF16),
            vmem((2, SHARD, D), BF16),
            vmem((D, CHIP), BF16),
            vmem((CHIP, QUERIES), F32),
            vmem((3, CHIP, QUERIES), BF16),
            vmem((NB, D, BATCH), F32),
            vmem((NB, D, BATCH), F32),
            vmem((NB, 2, D, UNIT), BF16),
            vmem((NB, 2, D, UNIT), BF16),
            vmem((NB, 2, D, UNIT), BF16),
            vmem((NB, 2, D, UNIT), BF16),
            vmem((NB, 2, D, UNIT), BF16),
            vmem((3, D, UNIT), BF16),
            vmem((D, UNIT), F32),
            vmem((SHARD, D), BF16),
            vmem((SHARD, D), BF16),
            vmem((SHARD, D), F32),
            vmem((NB, 8, BATCH), F32),
            vmem((NB, 3, 8, BATCH), F32),
            vmem((NB, 8, BATCH), F32),
            vmem((NB, 8, BATCH), F32),
            vmem((NB, 3, 8, BATCH), F32),
            vmem((NB, 8, BATCH), F32),
            vmem((NB, 8, BATCH), F32),
            vmem((NB, 8, BATCH), F32),
            vmem((NB, 8, BATCH), F32),
            vmem((8, UNIT), F32),
            vmem((8, UNIT), F32),
            dma((2 * NB + 1,)), dma((3,)), dma((3,)),
            dma((NB, PIECES)), dma((NB, PIECES)), dma((NB, PIECES)), dma((NB, PIECES)),
            dma((NB, 2, PIECES)), dma((NB, 2, PIECES)),
            dma((NB, 3)), dma((NB, 3)), dma((NB, 3)), dma((NB, 3)), dma((NB,)), dma((NB,)), dma((NB,)), dma((NB,)),
            dma((NB, 8)), dma((NB, 8)), dma((NB, 8)), dma((NB, 8)),
            dma((NB, 8)), dma((3, PARTS)),
        ],
        compiler_params=pltpu.CompilerParams(
            collective_id=0, has_side_effects=True, vmem_limit_bytes=52 * 1024 * 1024
        ),
        cost_estimate=pl.CostEstimate(
            flops=9 * 2 * 1024**3, bytes_accessed=7 * 2**20, transcendentals=3 * 2**20
        ),
    )(
        queries.reshape(4, 2, UNIT, D),
        passages,
        block_mask,
        positives.reshape(8, UNIT),
    )
    return loss.reshape(1024), query_grad, passage_grad


def solution(mesh):
    in_specs = (P("qgrp", None), P(("qgrp", "pcol"), None), P(), P("qgrp"))
    out_specs = (P("qgrp"), P(("qgrp", "pcol"), None), P(("qgrp", "pcol"), None))
    return jax.shard_map(
        on_device, mesh=mesh, in_specs=in_specs, out_specs=out_specs, check_vma=False
    )
```

```python
import functools

import jax
import jax.numpy as jnp
from jax import lax
from jax.experimental import pallas as pl
from jax.experimental.pallas import tpu as pltpu
from jax.sharding import PartitionSpec as P

F32 = jnp.float32
BF16 = jnp.bfloat16
D = 1024
SHARD = 1024
CHIP = 2048
UNIT = 128
BATCH = 256
QUERIES = 512
NB = 2
PIECES = 4
HALF = 512
PARTS = 4
PART = 256
ROWS = 256
LAST = D - PART
CHAIN = 2 * PARTS - 2
LOW = -1e30
MESH = pl.DeviceIdType.MESH


def dot_nt(a, b):
    return lax.dot_general(a, b, (((1,), (1,)), ((), ())), preferred_element_type=F32)


def dot_nn(a, b):
    return jnp.dot(a, b, preferred_element_type=F32)


def kernel(
    q_hbm, p_hbm, mask_ref, pos_ref,
    loss_ref, qg_ref, pg_ref,
    qv, pv, pt, lg, ev, t2, t1, t0,
    sb, rb, sa, ra, sy, ry, acc, zs, zr, za, zb, zc,
    pgs, pgr, pgo,
    st, sty, stm, stc, stx, sc, sd, sf, pas, par, ls, lr,
    load_sem, pair_send, pair_recv,
    qa_send, qa_recv, qb_send, qb_recv, qy_send, qy_recv,
    sty_send, sty_recv, stx_send, stx_recv, stm_send, stm_recv, pa_send, pa_recv,
    tb_send, tb_recv, ta_send, ta_recv, ty_send, ty_recv,
    z_send, z_recv, zx_send, zx_recv,
):
    g = lax.axis_index("qgrp")
    k = lax.axis_index("pcol")
    x = lax.rem(g, 4)
    y = lax.div(k, 2)
    c = lax.rem(k, 2)
    h = lax.rem(y, 2)
    g1 = g + 1 - 2 * lax.rem(x, 2)
    g2 = g + 2 - 4 * lax.div(x, 2)
    g3 = g + 3 - 2 * x
    up = (g, lax.rem(k + 2, 8))
    far = (g, lax.rem(k + 4, 8))
    down = (g, lax.rem(k + 6, 8))
    pair = (g, k + 1 - 2 * c)
    n1, n2, n3 = (g1, k), (g2, k), (g3, k)

    def rcopy(src, dst, ssem, rsem, dev):
        return pltpu.make_async_remote_copy(
            src_ref=src, dst_ref=dst, send_sem=ssem, recv_sem=rsem,
            device_id=dev, device_id_type=MESH,
        )

    loads = [pltpu.make_async_copy(p_hbm, pv.at[0], load_sem.at[NB * 2])]
    for b in range(NB):
        for j in range(2):
            slot = 2 * b + j
            loads.append(
                pltpu.make_async_copy(q_hbm.at[b + 2 * j, c], qv.at[0, slot], load_sem.at[slot])
            )
    for copy in loads:
        copy.start()

    barrier = pltpu.get_barrier_semaphore()
    for dev in (up, far, down, pair, n1, n2, n3):
        pl.semaphore_signal(barrier, inc=1, device_id=dev, device_id_type=MESH)
    pl.semaphore_wait(barrier, 7)

    p_swap = rcopy(p_hbm, pv.at[1], pair_send.at[0], pair_recv.at[0], pair)
    sends = [p_swap]

    def start(copy):
        copy.start()
        sends.append(copy)

    def rows(i):
        return pl.ds(64 * (i % 2) + 32 * (i // 2), 32)

    def qa(b, i):
        return rcopy(
            q_hbm.at[b + 2 * h, c, rows(i)], qv.at[1, 2 * b + h, rows(i)],
            qa_send.at[b, i], qa_recv.at[b, i], n1,
        )

    def qb(b, i):
        return rcopy(
            qv.at[1, 2 * b + h, rows(i)], qv.at[2, 2 * b + h, rows(i)],
            qb_send.at[b, i], qb_recv.at[b, i], n3,
        )

    def qy(b, r, i):
        block = qv.at[1 + r, 2 * b + h, rows(i)]
        return rcopy(
            block, block, qy_send.at[b, r, i], qy_recv.at[b, r, i], (up, down)[i % 2]
        )

    def qy_wait(b, r):
        for i in range(PIECES):
            block = qv.at[1 + r, 2 * b + 1 - h, rows(i)]
            rcopy(
                block, block, qy_send.at[b, r, i], qy_recv.at[b, r, i], (up, down)[i % 2]
            ).wait_recv()

    for b in range(NB):
        for i in range(PIECES):
            start(qa(b, i))
    p_swap.start()

    def forward_a(b, i):
        qa(b, i).wait_recv()
        start(qb(b, i))
        start(qy(b, 0, i))

    def forward_b(b, i):
        qb(b, i).wait_recv()
        start(qy(b, 1, i))

    flags = [mask_ref[0, g1] > 0, mask_ref[1, g2] > 0]

    def positive_row(b):
        return jnp.concatenate(
            [pos_ref[pl.ds(2 * (b + 2 * j) + c, 1), :] for j in range(2)], axis=1
        )

    def first_column(half):
        return (k if half == 0 else k + 1 - 2 * c) * SHARD

    ls[...] = jnp.zeros((8, UNIT), F32)
    for copy in loads:
        copy.wait()
    own_max = jnp.full((1, QUERIES), LOW, F32)

    def own_logits(half, peak):
        def body(i, peak):
            own_queries = qv[0].reshape(QUERIES, D)
            block = dot_nt(pv[half, pl.ds(i * 512, 512), :], own_queries)
            lg[pl.ds(half * SHARD + i * 512, 512), :] = block
            return jnp.maximum(peak, jnp.max(block, axis=0, keepdims=True))

        return lax.fori_loop(0, 2, body, peak)

    def transpose(half):
        for i in range(4):
            first = half * SHARD + i * 256
            pt[:, first:first + 256] = pv[half, pl.ds(i * 256, 256), :].T

    own_max = own_logits(0, own_max)
    transpose(0)
    forward_a(0, 0)
    p_swap.wait_recv()
    own_max = own_logits(1, own_max)
    forward_a(0, 1)
    forward_a(0, 2)
    transpose(1)
    forward_b(0, 0)
    forward_a(0, 3)

    positive_all = jnp.concatenate([positive_row(b) for b in range(NB)], axis=1)

    def own_exp(half, carry):
        def body(i, carry):
            total, positive = carry
            r = half * SHARD + i * 256
            block = lg[pl.ds(r, 256), :]
            column = lax.broadcasted_iota(jnp.int32, (256, QUERIES), 0) + (
                first_column(half) + i * 256
            )
            e = jnp.exp(block - own_max)
            ev[0, pl.ds(r, 256), :] = e.astype(BF16)
            total = total + jnp.sum(e, axis=0, keepdims=True)
            positive = positive + jnp.sum(
                jnp.where(column == positive_all, block, 0.0), axis=0, keepdims=True
            )
            return total, positive

        return lax.fori_loop(0, 4, body, carry)

    zero = jnp.zeros((1, QUERIES), F32)
    own_sums = own_exp(0, (zero, zero))
    forward_b(0, 1)
    forward_a(1, 0)
    own_total, own_positive = own_exp(1, own_sums)
    forward_b(0, 2)
    forward_a(1, 1)
    forward_b(0, 3)
    for b in range(NB):
        part = slice(b * BATCH, (b + 1) * BATCH)
        st[b, 0:1, :] = own_max[:, part]
        st[b, 3:4, :] = own_total[:, part]
        st[b, 6:7, :] = own_positive[:, part]
        st[b, 7:8, :] = jnp.zeros((1, BATCH), F32)

    def lent(b, r):
        def body(half, peak):
            queries = qv[1 + r, 2 * b:2 * b + 2].reshape(BATCH, D)
            block = dot_nt(pv[half], queries)
            lg[pl.ds(half * SHARD, SHARD), 0:BATCH] = block
            return jnp.maximum(peak, jnp.max(block, axis=0, keepdims=True))

        peak = lax.fori_loop(0, 2, body, jnp.full((1, BATCH), LOW, F32))

        def exp_body(i, total):
            e = jnp.exp(lg[pl.ds(i * 256, 256), 0:BATCH] - peak)
            ev[1 + r, pl.ds(i * 256, 256), b * BATCH:(b + 1) * BATCH] = e.astype(BF16)
            return total + jnp.sum(e, axis=0, keepdims=True)

        total = lax.fori_loop(0, 8, exp_body, jnp.zeros((1, BATCH), F32))
        st[b, 1 + r:2 + r, :] = jnp.where(flags[r], peak, LOW)
        st[b, 4 + r:5 + r, :] = total

    def stats_y(b, i):
        dev = (down, far, up)[i]
        return rcopy(st.at[b], sty.at[b, i], sty_send.at[b, i], sty_recv.at[b, i], dev)

    def stats_m(b):
        return rcopy(st.at[b], stm.at[b], stm_send.at[b], stm_recv.at[b], n3)

    def peak_a(b):
        return rcopy(pas.at[b], par.at[b], pa_send.at[b], pa_recv.at[b], n1)

    def pair_scale(b):
        stats_m(b).wait_recv()
        here, there = st[b, 1:2, :], stm[b, 2:3, :]
        peak = jnp.maximum(here, there)
        sd[b, 0:1, :] = jnp.exp(here - peak)
        sd[b, 1:2, :] = jnp.exp(there - peak)
        pas[b] = jnp.broadcast_to(peak, (8, BATCH))
        start(peak_a(b))

    def stats_x(b, i):
        dev = (n1, n2, n3)[i]
        return rcopy(stc.at[b], stx.at[b, i], stx_send.at[b, i], stx_recv.at[b, i], dev)

    def combine_y(b):
        for i in range(3):
            stats_y(b, i).wait_recv()
        peaks = [st[b, 0:3, :]] + [sty[b, i, 0:3, :] for i in range(3)]
        sums = [st[b, 3:6, :]] + [sty[b, i, 3:6, :] for i in range(3)]
        peak = functools.reduce(jnp.maximum, peaks)
        total = sum(s * jnp.exp(m - peak) for s, m in zip(sums, peaks))
        positive = st[b, 6:7, :] + sty[b, 0, 6:7, :] + sty[b, 1, 6:7, :] + sty[b, 2, 6:7, :]
        stc[b, 0:3, :] = peak
        stc[b, 3:6, :] = total
        stc[b, 6:7, :] = positive
        stc[b, 7:8, :] = jnp.zeros((1, BATCH), F32)

    def combine_x(b):
        for i in range(3):
            stats_x(b, i).wait_recv()
        own, one, two, three = stc[b], stx[b, 0], stx[b, 1], stx[b, 2]
        sources = (
            ((own, 0), (one, 1), (two, 2)),
            ((one, 0), (own, 1), (three, 2)),
            ((two, 0), (own, 2), (three, 1)),
        )
        log_totals = []
        for source in sources:
            peaks = [a[r:r + 1] for a, r in source]
            sums = [a[3 + r:4 + r] for a, r in source]
            peak = functools.reduce(jnp.maximum, peaks)
            total = sum(s * jnp.exp(m - peak) for s, m in zip(sums, peaks))
            log_totals.append(peak + jnp.log(total))
        for r in range(3):
            sc[b, r:r + 1, :] = jnp.exp(st[b, r:r + 1, :] - log_totals[r])
        peak_a(b).wait_recv()
        sc[b, 4:5, :] = jnp.exp(par[b, 0:1, :] - log_totals[0])
        here = jnp.exp(own[1:2] - log_totals[1])
        there = jnp.exp(three[2:3] - log_totals[1])
        for j in range(2):
            sf[b + 2 * j, 0:1, :] = here[:, j * UNIT:(j + 1) * UNIT]
            sf[b + 2 * j, 1:2, :] = there[:, j * UNIT:(j + 1) * UNIT]
        positive = own[6:7]
        sc[b, 3:4, :] = jnp.exp(positive - log_totals[0]) - 1.0
        loss = log_totals[0] - positive
        for j in range(2):
            ls[b + 2 * j:b + 2 * j + 1, :] = loss[:, j * UNIT:(j + 1) * UNIT]

    def term(b, r, i):
        return dot_nn(pt[pl.ds(i * HALF, HALF), :], ev[r, :, b * BATCH:(b + 1) * BATCH])

    def terms(b, r):
        target = t0 if r == 0 else t1

        @pl.loop(0, 2)
        def _(i):
            target[b, pl.ds(i * HALF, HALF), :] = term(b, r, i)

    def own_weights(b):
        scale, less = sc[b, 0:1, :], sc[b, 3:4, :]
        where = positive_row(b)
        for half in range(2):
            @pl.loop(0, 4)
            def _(i):
                span = pl.ds(half * SHARD + i * 256, 256)
                column = lax.broadcasted_iota(jnp.int32, (256, BATCH), 0) + (
                    first_column(half) + i * 256
                )
                e = ev[0, span, b * BATCH:(b + 1) * BATCH].astype(F32)
                w = jnp.where(column == where, less, e * scale)
                ev[0, span, b * BATCH:(b + 1) * BATCH] = w.astype(BF16)

    def lent_weights(b, r):
        scale = sc[b, 1 + r:2 + r, :]

        @pl.loop(0, 8)
        def _(i):
            span = pl.ds(i * 256, 256)
            e = ev[1 + r, span, b * BATCH:(b + 1) * BATCH].astype(F32)
            ev[1 + r, span, b * BATCH:(b + 1) * BATCH] = (e * scale).astype(BF16)

    def part(n):
        return n % 2, pl.ds(PART * (n // 2), PART)

    def tb(b, n):
        j, d = part(n)
        return rcopy(
            sb.at[b, j, d], rb.at[b, j, d], tb_send.at[b, n], tb_recv.at[b, n], n3
        )

    def ta(b, n):
        j, d = part(n)
        return rcopy(
            sa.at[b, j, d], ra.at[b, j, d], ta_send.at[b, n], ta_recv.at[b, n], n1
        )

    def ty(b, n):
        j, d = part(n)
        unit = b + 2 * j
        slot = lax.rem(y - unit + 4, 4) - 1
        return rcopy(
            sy.at[b, j, d], ry.at[slot, d], ty_send.at[b, n], ty_recv.at[slot, n // 2],
            (g, 2 * unit + c),
        )

    def lanes(j):
        return slice(j * UNIT, (j + 1) * UNIT)

    def make_b(b, i):
        total = term(b, 2, i)
        count = min(LAST - i * HALF, HALF)
        for j in range(2):
            sb[b, j, i * HALF:i * HALF + count, :] = total[:count, lanes(j)].astype(BF16)
        if count < HALF:
            t2[b] = total[count:, :]

    def send_b(b, *pieces):
        for n in pieces:
            start(tb(b, n))

    def send_a(b, n):
        j, d = part(n)
        tb(b, n).wait_recv()
        sa[b, j, d] = (
            t1[b, d, lanes(j)] * sd[b, 0:1, lanes(j)]
            + rb[b, j, d].astype(F32) * sd[b, 1:2, lanes(j)]
        ).astype(BF16)
        start(ta(b, n))

    def send_y(b, n):
        j, d = part(n)
        unit = b + 2 * j
        total = t0[b, d, lanes(j)]
        if n < CHAIN:
            ta(b, n).wait_recv()
            total = total + ra[b, j, d].astype(F32) * sc[b, 4:5, lanes(j)]

        @pl.when(y == unit)
        def _():
            acc[d] = total

        @pl.when(y != unit)
        def _():
            sy[b, j, d] = total.astype(BF16)
            ty(b, n).start()

    def ty_first(b, r, j):
        unit = b + 2 * j
        slot = lax.rem(y - unit + 4, 4) - 1
        return rcopy(
            zs.at[r, b, j], zr.at[r, slot], z_send.at[r, b, j], z_recv.at[r, slot],
            (g, 2 * unit + c),
        )

    def first_y(b):
        for r in (1, 0):
            scale = jnp.exp(st[b, 1 + r:2 + r, :] - stc[b, 1 + r:2 + r, :])
            total = (t1[b, LAST:, :] if r == 0 else t2[b]) * scale
            for j in range(2):
                @pl.when(y == b + 2 * j)
                def _():
                    za[r] = total[:, lanes(j)]

                @pl.when(y != b + 2 * j)
                def _():
                    zs[r, b, j] = total[:, lanes(j)].astype(BF16)
                    ty_first(b, r, j).start()

    def first_sum(r):
        total = za[r]
        for slot in range(3):
            rcopy(
                zs.at[r, 0, 0], zr.at[r, slot], z_send.at[r, 0, 0], z_recv.at[r, slot], up
            ).wait_recv()
            total = total + zr[r, slot].astype(F32)
        return total

    zx_b = rcopy(zb.at[0], zc.at[0], zx_send.at[0], zx_recv.at[0], n3)
    zx_a = rcopy(zb.at[1], zc.at[1], zx_send.at[1], zx_recv.at[1], n1)

    def first_b():
        zb[0] = first_sum(1).astype(BF16)
        start(zx_b)

    def first_a():
        total = first_sum(0) * sf[y, 0:1, :]
        zx_b.wait_recv()
        zb[1] = (total + zc[0].astype(F32) * sf[y, 1:2, :]).astype(BF16)
        start(zx_a)

    def passage_part(half, i, target):
        total = None
        for r in range(3):
            add = dot_nn(
                ev[r, pl.ds(half * SHARD + i * ROWS, ROWS), :], qv[r].reshape(QUERIES, D)
            )
            total = add if total is None else total + add
        target[pl.ds(i * ROWS, ROWS), :] = total.astype(target.dtype)

    def begin_stats(b):
        start(stats_m(b))
        for i in range(3):
            start(stats_y(b, i))

    def begin_stats_x(b):
        combine_y(b)
        for i in range(3):
            start(stats_x(b, i))

    def send_a_all(b, *pieces):
        for n in pieces:
            send_a(b, n)

    def send_y_all(b, *pieces):
        for n in pieces:
            send_y(b, n)

    forward_a(1, 2)
    qy_wait(0, 0)
    lent(0, 0)
    forward_b(1, 0)
    forward_a(1, 3)
    forward_b(1, 1)
    qy_wait(0, 1)
    lent(0, 1)
    begin_stats(0)
    make_b(0, 0)
    send_b(0, 0, 1, 2, 3)
    forward_b(1, 2)
    make_b(0, 1)
    forward_b(1, 3)
    terms(0, 1)
    qy_wait(1, 0)
    lent(1, 0)
    begin_stats_x(0)
    send_b(0, 4, 5)
    pair_scale(0)
    send_a_all(0, 0)
    first_y(0)
    qy_wait(1, 1)
    lent(1, 1)
    begin_stats(1)
    make_b(1, 0)
    send_b(1, 0, 1)
    send_a_all(0, 1, 2, 3)
    make_b(1, 1)
    send_a_all(0, 4)
    combine_x(0)
    send_a_all(0, 5)
    own_weights(0)
    terms(0, 0)
    begin_stats_x(1)
    send_b(1, 2, 3, 4, 5)
    pair_scale(1)
    send_y_all(0, 0, 1, 2, 3)
    terms(1, 1)
    first_y(1)
    send_a_all(1, 0)
    send_y_all(0, 4, 5, 6, 7)
    send_a_all(1, 1)
    lent_weights(0, 0)
    lent_weights(0, 1)
    send_a_all(1, 2)
    first_b()
    combine_x(1)
    loss_copy = rcopy(ls, lr, pair_send.at[1], pair_recv.at[1], pair)
    start(loss_copy)
    own_weights(1)
    send_a_all(1, 3)
    terms(1, 0)
    send_a_all(1, 4, 5)
    send_y_all(1, 6, 7, 0, 1)
    lent_weights(1, 0)
    lent_weights(1, 1)
    passage_part(1, 0, pgs)
    send_y_all(1, 2)
    first_a()
    passage_part(1, 1, pgs)
    send_y_all(1, 3)
    passage_part(1, 2, pgs)
    send_y_all(1, 4)
    send_y_all(1, 5)
    passage_part(1, 3, pgs)
    pg_copy = rcopy(pgs, pgr, pair_send.at[2], pair_recv.at[2], pair)
    start(pg_copy)
    passage_part(0, 0, pgo)
    passage_part(0, 1, pgo)
    passage_part(0, 2, pgo)
    passage_part(0, 3, pgo)
    loss_copy.wait_recv()
    for j in range(4):
        loss_ref[pl.ds(2 * j + c, 1), :] = ls[j:j + 1, :]
        loss_ref[pl.ds(2 * j + 1 - c, 1), :] = lr[j:j + 1, :]
    pg_copy.wait_recv()
    for i in range(4):
        span = pl.ds(i * 256, 256)
        pg_ref[span, :] = (pgo[span, :] + pgr[span, :].astype(F32)).astype(BF16)
    for i in range(PARTS):
        d = slice(i * PART, (i + 1) * PART)
        total = acc[d]
        for slot in range(3):
            rcopy(
                sy.at[0, 0, d], ry.at[slot, d], ty_send.at[0, 0], ty_recv.at[slot, i], up
            ).wait_recv()
            total = total + ry[slot, d].astype(F32)
        if i == PARTS - 1:
            zx_a.wait_recv()
            total = total + zc[1].astype(F32)
        qg_ref[:, d] = total.T.astype(BF16)
    for copy in sends:
        copy.wait_send()
    for b in range(NB):
        for n in range(2 * PARTS):
            @pl.when(y != b + 2 * (n % 2))
            def _():
                ty(b, n).wait_send()
        for j in range(2):
            @pl.when(y != b + 2 * j)
            def _():
                for r in range(2):
                    ty_first(b, r, j).wait_send()


def on_device(queries, passages, block_mask, positives):
    vmem = pltpu.VMEM
    dma = pltpu.SemaphoreType.DMA
    loss, query_grad, passage_grad = pl.pallas_call(
        kernel,
        out_shape=(
            pltpu.VMEM((8, 128), F32),
            pltpu.VMEM((UNIT, D), BF16),
            pltpu.VMEM((SHARD, D), BF16),
        ),
        in_specs=[
            pl.BlockSpec(memory_space=pl.ANY),
            pl.BlockSpec(memory_space=pl.ANY),
            pl.BlockSpec(memory_space=pltpu.SMEM),
            pl.BlockSpec(memory_space=pltpu.VMEM),
        ],
        out_specs=(
            pl.BlockSpec(memory_space=pltpu.VMEM),
            pl.BlockSpec(memory_space=pltpu.VMEM),
            pl.BlockSpec(memory_space=pltpu.VMEM),
        ),
        scratch_shapes=[
            vmem((3, 4, UNIT, D), BF16),
            vmem((2, SHARD, D), BF16),
            vmem((D, CHIP), BF16),
            vmem((CHIP, QUERIES), F32),
            vmem((3, CHIP, QUERIES), BF16),
            vmem((NB, PART, BATCH), F32),
            vmem((NB, D, BATCH), F32),
            vmem((NB, D, BATCH), F32),
            vmem((NB, 2, D, UNIT), BF16),
            vmem((NB, 2, D, UNIT), BF16),
            vmem((NB, 2, D, UNIT), BF16),
            vmem((NB, 2, D, UNIT), BF16),
            vmem((NB, 2, D, UNIT), BF16),
            vmem((3, D, UNIT), BF16),
            vmem((D, UNIT), F32),
            vmem((2, NB, 2, PART, UNIT), BF16),
            vmem((2, 3, PART, UNIT), BF16),
            vmem((2, PART, UNIT), F32),
            vmem((2, PART, UNIT), BF16),
            vmem((2, PART, UNIT), BF16),
            vmem((SHARD, D), BF16),
            vmem((SHARD, D), BF16),
            vmem((SHARD, D), F32),
            vmem((NB, 8, BATCH), F32),
            vmem((NB, 3, 8, BATCH), F32),
            vmem((NB, 8, BATCH), F32),
            vmem((NB, 8, BATCH), F32),
            vmem((NB, 3, 8, BATCH), F32),
            vmem((NB, 8, BATCH), F32),
            vmem((NB, 8, BATCH), F32),
            vmem((4, 8, UNIT), F32),
            vmem((NB, 8, BATCH), F32),
            vmem((NB, 8, BATCH), F32),
            vmem((8, UNIT), F32),
            vmem((8, UNIT), F32),
            dma((2 * NB + 1,)), dma((3,)), dma((3,)),
            dma((NB, PIECES)), dma((NB, PIECES)), dma((NB, PIECES)), dma((NB, PIECES)),
            dma((NB, 2, PIECES)), dma((NB, 2, PIECES)),
            dma((NB, 3)), dma((NB, 3)), dma((NB, 3)), dma((NB, 3)), dma((NB,)), dma((NB,)), dma((NB,)), dma((NB,)),
            dma((NB, 8)), dma((NB, 8)), dma((NB, 8)), dma((NB, 8)),
            dma((NB, 8)), dma((3, PARTS)),
            dma((2, NB, 2)), dma((2, 3)), dma((2,)), dma((2,)),
        ],
        compiler_params=pltpu.CompilerParams(
            collective_id=0, has_side_effects=True, vmem_limit_bytes=52 * 1024 * 1024
        ),
        cost_estimate=pl.CostEstimate(
            flops=9 * 2 * 1024**3, bytes_accessed=7 * 2**20, transcendentals=3 * 2**20
        ),
    )(
        queries.reshape(4, 2, UNIT, D),
        passages,
        block_mask,
        positives.reshape(8, UNIT),
    )
    return loss.reshape(1024), query_grad, passage_grad


def solution(mesh):
    in_specs = (P("qgrp", None), P(("qgrp", "pcol"), None), P(), P("qgrp"))
    out_specs = (P("qgrp"), P(("qgrp", "pcol"), None), P(("qgrp", "pcol"), None))
    return jax.shard_map(
        on_device, mesh=mesh, in_specs=in_specs, out_specs=out_specs, check_vma=False
    )
```
